512 devices in a mesh: tm: 128 (over z_hi, y, x, core), tmpl: 4 (over z_lo).
Axes of the slice: x: 4, y: 8, z: 8 (z_hi: 2, z_lo: 4; z = z_hi * 4 + z_lo), core: 2. Of those that a mesh axis runs over, the one named last changes fastest.
Arguments:
- records: bfloat16 [1024, 49152], P(None, 'tm'), may hold values from -6 to 6
- templates: bfloat16 [4, 1024, 300], P('tmpl', 'tm'), may hold values from -6 to 6
- shifts: int32 [4, 1024], P('tmpl', 'tm'), may hold values from 0 to 20, as said below
- valid: int32 [4, 1024], P('tmpl', 'tm'), may hold values 0 or 1
Outputs:
- stack: float32 [4, 49152], P('tmpl', 'tm')
The draws below stay inside these ranges and needn't reach their ends.
Inputs may be any that keep to these rules, and one draw needn't show every extreme that they name: `shifts`: every template has some channel with shift 0 and some channel with shift 20.
All inputs are finite; a program needn't handle non-finite values. No bound on the sum of `valid` on one device may be relied on, other than what follows from the above.
Results may differ from the reference program's by a relative error of at most 0.004.
Values may be sent and summed in bfloat16 or wider, within the bound.
A program may use at most 64 MiB of HBM per device.

```python
import jax
import jax.numpy as jnp
from jax import lax

CH = 1024
L = 300
MAXS = 20
K = 4
NT = 49152


def draw_shifts(key, part):
    first, second, third = jax.random.split(jax.random.fold_in(key, 17), 3)
    raw = jax.random.randint(first, (K, CH), 0, MAXS + 1)
    lowest = jax.random.randint(second, (K, 1), 0, CH)
    highest = (lowest + 1 + jax.random.randint(third, (K, 1), 0, CH - 1)) % CH
    column = jnp.arange(CH)[None, :]
    raw = jnp.where(column == lowest, 0, raw)
    raw = jnp.where(column == highest, MAXS, raw)
    return raw.astype(jnp.int32)


def with_ends(values, rng, low, largest):
    longest = values.shape.index(max(values.shape))
    spots = []
    for shift in (0, 1):
        where = [jax.random.randint(jax.random.fold_in(rng, axis), (), 0, length) for axis, length in enumerate(values.shape)]
        where[longest] = (where[longest] + shift) % values.shape[longest]
        spots.append(tuple(where))
    return values.at[spots[0]].set(low).at[spots[1]].set(largest)


def block_scale(key, shape, pieces, smallest, high):
    def one(axis_at, blocks):
        heights = jax.random.uniform(jax.random.fold_in(jax.random.fold_in(key, 6), axis_at), (blocks,), jnp.float32, smallest / len(pieces), high / len(pieces))
        return jnp.repeat(jnp.exp(heights), shape[axis_at] // blocks).reshape((-1,) + (1,) * (len(shape) - axis_at - 1))

    factor_of = one(*pieces[0])
    for cut in pieces[1:]:
        factor_of = factor_of * one(*cut)
    return factor_of


def bell_draw(rng, dims, spread, limit, pieces=(), kind=jnp.bfloat16):
    gain = block_scale(rng, dims, pieces, -0.22, 0.18) if pieces else 1.0
    drawn = jax.random.normal(rng, dims, jnp.float32) * spread * gain
    return jnp.minimum(jnp.maximum(drawn, -limit), limit).astype(kind)


def setup_inputs(seed: int = 0) -> dict:
    splits = jax.random.split(jax.random.key(seed), 5)
    records = bell_draw(splits[0], (CH, NT), 1.0, 6.0, ((1, 128),))
    templates = bell_draw(splits[1], (K, CH, L), 1.0, 6.0, ((0, 4), (1, 128)))
    shifts = draw_shifts(jax.random.fold_in(splits[4], 71), 0)
    valid = with_ends((jax.random.randint(splits[3], (K, CH), 0, 4) < 3).astype(jnp.int32), jax.random.fold_in(splits[3], 1), 0, 1)
    return dict(records=records, templates=templates, shifts=shifts, valid=valid)


eps = 1e-05

def window_energy(rows):
    squares = rows.astype(jnp.float32) ** 2
    running = jnp.concatenate([jnp.zeros((rows.shape[0], 1), jnp.float32), jnp.cumsum(squares, axis=1)], axis=1)
    return jnp.maximum(running[:, L:] - running[:, :-L], 0.0) / L

def correlate_block(rows, waves, moves, masks):
    count = rows.shape[0]
    kinds = waves.shape[0]
    span = rows.shape[1] - L + 1
    length = span - MAXS
    kernel = jnp.transpose(waves, (1, 0, 2)).reshape(count * kinds, 1, L)
    corr = lax.conv_general_dilated(rows[None], kernel, (1,), 'VALID', dimension_numbers=('NCH', 'OIH', 'NCH'), feature_group_count=count, preferred_element_type=jnp.float32)[0].reshape(count, kinds, span)
    energy = window_energy(rows)
    power = lax.optimization_barrier(jnp.mean(waves.astype(jnp.float32) ** 2, axis=2)).T
    weight = masks.T.astype(jnp.float32) / (L * jnp.sqrt(power + eps))
    normed = corr / jnp.sqrt(energy + eps)[:, None, :] * weight[:, :, None]
    picked = jax.vmap(jax.vmap(lambda row, move: lax.dynamic_slice_in_dim(row, move, length)))(normed, moves.T.astype(jnp.int32))
    return lax.optimization_barrier(jnp.sum(picked, axis=0))

def reference(records, templates, shifts, valid):
    channels = records.shape[0]
    kinds = templates.shape[0]
    padded = jnp.concatenate([records, jnp.zeros((channels, L - 1 + MAXS), jnp.bfloat16)], axis=1)
    block = max((d for d in range(1, 25) if channels % d == 0))
    blocks = channels // block
    rows_all = padded.reshape(blocks, block, padded.shape[1])
    waves_all = jnp.moveaxis(templates.reshape(kinds, blocks, block, L), 1, 0)
    moves_all = jnp.moveaxis(shifts.reshape(kinds, blocks, block), 1, 0)
    masks_all = jnp.moveaxis(valid.reshape(kinds, blocks, block), 1, 0)

    def step(total, items):
        return (total + correlate_block(*items), None)
    total, _ = lax.scan(step, jnp.zeros((kinds, records.shape[1]), jnp.float32), (rows_all, waves_all, moves_all, masks_all))
    return total
```

```python
import jax
import jax.numpy as jnp
from jax import lax
from jax.sharding import PartitionSpec as P

L = 300
MAXS = 20


eps = 1e-05


def from_behind(array, axis, by):
    devices = lax.axis_size(axis)
    pairs = [(i, i + by) for i in range(devices) if 0 <= i + by < devices]
    return lax.ppermute(array, axis, pairs)


def running16(parts):
    acc = [parts[..., 0]]
    for i in range(1, 16):
        acc.append(acc[-1] + parts[..., i])
    return jnp.stack(acc, axis=-1)


def prefix(items):
    count = items.shape[1]
    if count <= 16:
        acc = [items[:, 0]]
        for i in range(1, count):
            acc.append(acc[-1] + items[:, i])
        return jnp.stack(acc, axis=1)
    inner = running16(items.reshape(items.shape[0], count // 16, 16))
    outer = prefix(inner[:, :, 15])
    before = jnp.concatenate([jnp.zeros_like(outer[:, :1]), outer[:, :-1]], axis=1)
    return (inner + before[:, :, None]).reshape(items.shape)


def window_energy(extended):
    channels, wide = extended.shape
    squares = extended.astype(jnp.float32) ** 2
    squares = jnp.concatenate([squares, jnp.zeros((channels, 1), jnp.float32)], axis=1)
    inner = running16(squares.reshape(channels, (wide + 1) // 16, 16))
    mine = (wide - (L - 1 + MAXS)) // 16
    totals = lax.all_gather(inner[:, :mine, 15], "tm", axis=1, tiled=True)
    totals = jnp.concatenate([totals, jnp.zeros((channels, 256), jnp.float32)], axis=1)
    outer = prefix(totals)
    outer = jnp.concatenate([jnp.zeros((channels, 2), jnp.float32), outer], axis=1)
    totals = jnp.concatenate([jnp.zeros((channels, 1), jnp.float32), totals], axis=1)
    first = lax.axis_index("tm") * mine
    before = lax.dynamic_slice_in_dim(outer, first + 1, inner.shape[1], 1)
    last = lax.dynamic_slice_in_dim(outer, first, 1, 1) + lax.dynamic_slice_in_dim(totals, first, 1, 1)
    running = (inner + before[:, :, None]).reshape(channels, wide + 1)[:, :wide]
    running = jnp.concatenate([last, running], axis=1)
    return jnp.maximum(running[:, L:] - running[:, :-L], 0.0) / L


def correlate_block(rows, energy, waves, moves, masks):
    count = rows.shape[0]
    kinds = waves.shape[0]
    span = rows.shape[1] - L + 1
    length = span - MAXS
    kernel = jnp.transpose(waves, (1, 0, 2)).reshape(count * kinds, 1, L)
    corr = lax.conv_general_dilated(
        rows[None],
        kernel,
        (1,),
        "VALID",
        dimension_numbers=("NCH", "OIH", "NCH"),
        feature_group_count=count,
        preferred_element_type=jnp.float32,
    )[0].reshape(count, kinds, span)
    power = jnp.mean(waves.astype(jnp.float32) ** 2, axis=2).T
    weight = masks.T.astype(jnp.float32) / (L * jnp.sqrt(power + eps))
    normed = corr / jnp.sqrt(energy + eps)[:, None, :] * weight[:, :, None]
    levels = jnp.arange(MAXS + 1, dtype=jnp.int32)
    selector = (moves.T.astype(jnp.int32)[None, :, :] == levels[:, None, None]).astype(jnp.float32)
    by_shift = jnp.einsum("sck,ckt->skt", selector, normed, precision=lax.Precision.HIGHEST)
    result = by_shift[0, :, 0:length]
    for level in range(1, MAXS + 1):
        result = result + by_shift[level, :, level : level + length]
    return result


def make_folder(source, energy, total, pieces, start):
    waves, moves, masks = pieces
    count = waves.shape[1]
    block = max((d for d in range(1, 129) if count % d == 0))

    def one_block(index, acc):
        offset = index * block
        rows = lax.dynamic_slice_in_dim(source, start + offset, block, 0)
        part_energy = lax.dynamic_slice_in_dim(energy, start + offset, block, 0)
        part_waves = lax.dynamic_slice_in_dim(waves, offset, block, 1)
        part_moves = lax.dynamic_slice_in_dim(moves, offset, block, 1)
        part_masks = lax.dynamic_slice_in_dim(masks, offset, block, 1)
        return acc + correlate_block(rows, part_energy, part_waves, part_moves, part_masks)

    return lax.fori_loop(0, count // block, one_block, total)


def local(records, templates, shifts, valid):
    channels, samples = records.shape
    width = L - 1 + MAXS
    leading = records[:, :width]
    trailing = from_behind(leading, "tm", -1)
    extended = jnp.concatenate([records, trailing], axis=1)
    start_total = jnp.zeros((templates.shape[0], samples), jnp.float32)
    stack = make_folder(
        extended,
        window_energy(extended),
        start_total,
        (
            lax.all_gather(templates, "tm", axis=1, tiled=True),
            lax.all_gather(shifts, "tm", axis=1, tiled=True),
            lax.all_gather(valid, "tm", axis=1, tiled=True),
        ),
        jnp.int32(0),
    )
    return stack


def solution(mesh):
    in_specs = (P(None, "tm"), P("tmpl", "tm", None), P("tmpl", "tm"), P("tmpl", "tm"))
    out_specs = P("tmpl", "tm")
    return jax.shard_map(local, mesh=mesh, in_specs=in_specs, out_specs=out_specs, check_vma=False)
```

```python
import functools

import jax
import jax.numpy as jnp
from jax import lax
from jax.experimental import pallas as pl
from jax.experimental.pallas import tpu as pltpu
from jax.sharding import PartitionSpec as P

L = 300
MAXS = 20
EPS = 1e-05
KINDS = 4
RING = 8
GROUPS = 16
PIECE = 384
ROWS = 32
OCT = 8
SETS = ROWS // OCT
STEP = 32
SPAN = RING * PIECE
WIDE = SPAN + PIECE
NH = 3584
NZ = 3328
BIG = 3 * 256
LEVELS = 22
BLOCKS = (WIDE // 16)
CHAIN = 208

f32 = jnp.float32
bf16 = jnp.bfloat16


def prepare(message, a_ref):
    pairs = SETS * KINDS * OCT
    low = message[:, :OCT, :].reshape(pairs, 256)
    high = message[:, OCT:, :].reshape(pairs, 256)

    parts = [low[:, :128].astype(bf16), low[:, 128:].astype(bf16), high[:, :128].astype(bf16)]
    lane = lax.broadcasted_iota(jnp.int32, (128, 256), 1)
    line = lax.broadcasted_iota(jnp.int32, (128, 256), 0)
    same = (lane % OCT) == (line % OCT)
    for u_lo in range(4):
        spread = jnp.where(line == STEP * u_lo + lane // OCT, 1.0, 0.0).astype(bf16)
        for u_hi in range(3):
            wide = jnp.dot(parts[u_hi], spread, preferred_element_type=f32)
            block = jnp.where(same, wide, 0.0).astype(bf16)
            for j in range(SETS):
                a_ref[j, 32 * u_lo : 32 * u_lo + 32, 256 * u_hi : 256 * u_hi + 256] = block[32 * j : 32 * j + 32]

    shift = high[:, 128:129]
    valid = high[:, 129:130]
    column = lax.broadcasted_iota(jnp.int32, (pairs, 128), 1)
    squares = low[:, :128] ** 2 + low[:, 128:] ** 2 + high[:, :128] ** 2
    power = jnp.sum(squares, axis=1, keepdims=True) / L
    weight = valid / (L * jnp.sqrt(power + EPS))

    kind = (lax.broadcasted_iota(jnp.int32, (pairs, 128), 0) // OCT) % KINDS
    picked = (shift == (column // KINDS).astype(f32)) & (kind == column % KINDS)
    sel = jnp.transpose(jnp.where(picked, 1.0, 0.0)).astype(bf16)
    return jnp.concatenate([sel, sel], axis=1)[: 4 * LEVELS], weight


def correlate(j, x, h_ref, a_ref, z_ref, corr_ref):
    x8 = jnp.concatenate([x[OCT * j : OCT * j + OCT], jnp.zeros((OCT, NH - WIDE), f32)], axis=1)
    slot = j % 2
    for i in range(STEP // 2):
        first = x8 if i == 0 else pltpu.roll(x8, NH - 2 * i, 1)
        second = pltpu.roll(x8, NH - 2 * i - 1, 1)
        h_ref[slot, 16 * i : 16 * i + 16, :] = jnp.concatenate([first, second], axis=0).astype(bf16)
    for n in range(NZ // 256):
        acc = None
        for u_hi in range(3):
            part = jnp.dot(
                a_ref[j, :, 256 * u_hi : 256 * u_hi + 256],
                h_ref[slot, :, 256 * n + 128 * u_hi : 256 * n + 128 * u_hi + 256],
                preferred_element_type=f32,
            )
            acc = part if acc is None else acc + part
        z_ref[slot, :, 256 * n : 256 * n + 256] = acc
    for k in range(KINDS):
        corr = z_ref[slot, 8 * k : 8 * k + 8, :]
        for u_lo in range(1, 4):
            corr = corr + pltpu.roll(z_ref[slot, 32 * u_lo + 8 * k : 32 * u_lo + 8 * k + 8, :], NZ - STEP * u_lo, 1)
        corr_ref[32 * j + 8 * k : 32 * j + 8 * k + 8, :] = corr


def block_sums(x, run_ref, sum_ref):
    squares = x * x
    quarter = SPAN // 4
    stacked = jnp.concatenate([squares[:, quarter * s : quarter * s + quarter] for s in range(4)], axis=0)
    halo = jnp.concatenate([squares[:, SPAN:], jnp.zeros((128 - ROWS, PIECE), f32)], axis=0)
    for i in range(quarter // 128):
        run_ref[128 * i : 128 * i + 128, :] = jnp.transpose(stacked[:, 128 * i : 128 * i + 128])
    for i in range(PIECE // 128):
        run_ref[quarter + 128 * i : quarter + 128 * i + 128, :] = jnp.transpose(halo[:, 128 * i : 128 * i + 128])
    rows = (quarter + PIECE) // 16
    acc = run_ref[pl.ds(0, rows, stride=16), :]
    for d in range(1, 16):
        acc = acc + run_ref[pl.ds(d, rows, stride=16), :]
        run_ref[pl.ds(d, rows, stride=16), :] = acc
    sum_ref[:rows, :] = acc
    sum_ref[rows:, :] = jnp.zeros((128 - rows, 128), f32)
    final = acc[quarter // 16 - 1 : quarter // 16]
    acc = sum_ref[pl.ds(0, 8, stride=16), :]
    for c in range(1, 16):
        acc = acc + sum_ref[pl.ds(c, 8, stride=16), :]
        sum_ref[pl.ds(c, 8, stride=16), :] = acc
    before = sum_ref[quarter // 16 - 2 : quarter // 16 - 1, :]
    return jnp.concatenate([acc[:3], final, before, jnp.zeros((3, 128), f32)], axis=0)


def window_energy(group, all_ref, run_ref, sum_ref, chain_ref, outer_ref, edge_ref, part_ref):
    for g in range(GROUPS):
        totals = all_ref[g]
        for s in range(4):
            moved = totals if s == 0 else pltpu.roll(totals, 128 - ROWS * s, 1)
            chain_ref[12 * g + 3 * s : 12 * g + 3 * s + 3, :] = moved[:3]
    chain_ref[12 * GROUPS :, :] = jnp.zeros((256 - 12 * GROUPS, 128), f32)
    plain = chain_ref[:CHAIN, :]
    acc = chain_ref[pl.ds(0, 16, stride=16), :]
    for b in range(1, 16):
        acc = acc + chain_ref[pl.ds(b, 16, stride=16), :]
        chain_ref[pl.ds(b, 16, stride=16), :] = acc
    outer_ref[:8, :] = jnp.zeros((8, 128), f32)
    top = jnp.zeros((1, 128), f32)
    for a in range(CHAIN // 16):
        outer_ref[16 * a + 9 : 16 * a + 25, :] = chain_ref[16 * a : 16 * a + 16, :] + top
        top = top + acc[a : a + 1]
    outer_ref[8:9, :] = jnp.zeros((1, 128), f32)
    edge_ref[:8, :] = jnp.zeros((8, 128), f32)
    edge_ref[9 : 9 + CHAIN, :] = plain + outer_ref[8 : 8 + CHAIN, :]
    edge_ref[8:9, :] = jnp.zeros((1, 128), f32)
    mine = outer_ref[7:23, :]
    edge = edge_ref[7:23, :]
    for g in range(1, GROUPS):
        here = group == g
        mine = jnp.where(here, outer_ref[12 * g + 7 : 12 * g + 23, :], mine)
        edge = jnp.where(here, edge_ref[12 * g + 7 : 12 * g + 23, :], edge)
    lane = lax.broadcasted_iota(jnp.int32, (1, 128), 1) // ROWS

    def spread(rows, b):
        out = rows[1 + b : 2 + b]
        for s in range(1, 4):
            out = jnp.where(lane == s, pltpu.roll(rows[1 + 3 * s + b : 2 + 3 * s + b], ROWS * s, 1), out)
        return out

    befores = [spread(mine, b) for b in range(3)] + [mine[13:14], mine[14:15]]
    edges = [spread(edge, b) for b in range(3)] + [edge[13:14], edge[14:15]]
    for b in range(5):
        part_ref[16 * b + 1 : 16 * b + 17, :] = sum_ref[16 * b : 16 * b + 16, :] + befores[b]
        part_ref[16 * b : 16 * b + 1, :] = edges[b]
    quarter = SPAN // 4
    rows = (quarter + PIECE) // 16
    base = part_ref[:rows, :]
    for d in range(16):
        run_ref[pl.ds(d, rows, stride=16), :] = run_ref[pl.ds(d, rows, stride=16), :] + base
    ahead = pltpu.roll(all_ref[jnp.maximum(group - 1, 0)], ROWS, 1)
    last = jnp.where(group > 0, ahead[3:4] + (ahead[4:5] + mine[0:1]), 0.0)
    stretch = quarter + PIECE
    run_ref[stretch : stretch + 128, :] = jnp.concatenate([jnp.zeros((127, 128), f32), last], axis=0)
    main = jnp.concatenate(
        [jnp.transpose(run_ref[128 * i : 128 * i + 128, :]) for i in range(quarter // 128)], axis=1
    )
    tail = [jnp.transpose(run_ref[quarter + 128 * i : quarter + 128 * i + 128, :])[:ROWS] for i in range(4)]
    running = jnp.concatenate([main[ROWS * s : ROWS * s + ROWS] for s in range(4)] + tail, axis=1)
    energy = pltpu.roll(running, NH - (L - 1), 1) - pltpu.roll(running, 1, 1)
    return jnp.maximum(energy, 0.0)[:, :NZ] / L


def stacked(inverse, weight, sel, corr_ref, n_ref, z_ref):
    pairs = SETS * KINDS * OCT
    for j in range(SETS):
        for k in range(KINDS):
            row = 32 * j + 8 * k
            corr_ref[row : row + 8, :] = corr_ref[row : row + 8, :] * inverse[OCT * j : OCT * j + OCT] * weight[row : row + 8]
        normed = corr_ref[32 * j : 32 * j + 32, :]
        head = normed.astype(bf16)
        n_ref[32 * j : 32 * j + 32, :] = head
        n_ref[pairs + 32 * j : pairs + 32 * j + 32, :] = (normed - head.astype(f32)).astype(bf16)
    for n in range(NZ // 256):
        z_ref[0, : 4 * LEVELS, 256 * n : 256 * n + 256] = jnp.dot(
            sel, n_ref[:, 256 * n : 256 * n + 256], preferred_element_type=f32
        )
    total = z_ref[0, :8, :]
    for i in range(1, LEVELS // 2):
        total = total + pltpu.roll(z_ref[0, 8 * i : 8 * i + 8, :], NZ - 2 * i, 1)
    return total + pltpu.roll(pltpu.roll(total, NZ - 1, 1), 4, 0)


def kernel(
    rec_ref, tmpl_ref, shift_ref, valid_ref, out_ref,
    xbuf, wbuf, msg, all_ref, part, land, half, full,
    h_ref, a_ref, z_ref, n_ref, corr_ref, run_ref, sum_ref, chain_ref, outer_ref, edge_ref, part_ref,
    w_send, w_recv, f_send, f_recv, x_send, x_recv, h_send, s_send, s_recv, g_send, g_recv,
    p_send, p_recv, q_send, q_recv, own,
):
    m, q = lax.axis_index("tm"), lax.axis_index("tmpl")
    group, r = m // RING, m % RING
    outer, inner = group // 4, group % 4
    dest_r, dest_q = (m // SETS) % RING, m // ROWS
    lies_here = (r == dest_r) & (q == dest_q) & (inner == m % SETS)
    head = (r == 0) & (group > 0)
    barrier = pltpu.get_barrier_semaphore()

    def signal(tm, tmpl):
        pl.semaphore_signal(barrier, inc=1, device_id=(tm, tmpl), device_id_type=pl.DeviceIdType.MESH)

    def remote(src, dst, send, recv, tm, tmpl):
        return pltpu.make_async_remote_copy(
            src_ref=src, dst_ref=dst, send_sem=send, recv_sem=recv,
            device_id=(tm, tmpl), device_id_type=pl.DeviceIdType.MESH,
        )

    def each(count, skip, step):
        for i in range(count):
            pl.when(i != skip)(functools.partial(step, i))

    source = ROWS * q + SETS * r + inner
    for k in range(KINDS):
        pl.when(jnp.logical_not((source == m) & (q == k)))(functools.partial(signal, source, k))
    each(4, outer, lambda i: signal((4 * i + inner) * RING + r, q))
    each(4, inner, lambda i: signal((4 * outer + i) * RING + r, q))
    each(RING, r, lambda i: signal(group * RING + i, q))
    each(KINDS, q, lambda i: signal(m, i))

    @pl.when(group < GROUPS - 1)
    def _():
        signal((group + 1) * RING, q)

    local = pltpu.make_async_copy(rec_ref.at[pl.ds(ROWS * (q * RING + r), ROWS), :], xbuf.at[r], own)
    local.start()

    waves = tmpl_ref[0].astype(f32)
    eye = lax.broadcasted_iota(jnp.int32, (OCT, OCT), 0) == lax.broadcasted_iota(jnp.int32, (OCT, OCT), 1)
    moves = jnp.sum(jnp.where(eye, shift_ref[...].astype(f32), 0.0), axis=1, keepdims=True)
    masks = jnp.sum(jnp.where(eye, valid_ref[...].astype(f32), 0.0), axis=1, keepdims=True)
    lane = lax.broadcasted_iota(jnp.int32, (OCT, 128), 1)
    extra = jnp.where(lane == 0, moves, jnp.where(lane == 1, masks, 0.0))
    tail = jnp.concatenate([waves[:, 256:], jnp.zeros((OCT, 128 - (L - 256)), f32)], axis=1)
    msg[...] = jnp.concatenate([waves[:, :256], jnp.concatenate([tail, extra], axis=1)], axis=0).astype(bf16)

    @pl.when(group == GROUPS - 1)
    def _():
        xbuf[RING] = jnp.zeros((ROWS, PIECE), bf16)

    count = 4 - lies_here.astype(jnp.int32) + 3 + 3 + (RING - 1) + (KINDS - 1) + RING * head.astype(jnp.int32)
    pl.semaphore_wait(barrier, count)

    def record(i):
        return rec_ref.at[pl.ds(ROWS * (q * RING + i), ROWS), :]

    slot = (m % SETS) * KINDS + q
    mine = pl.ds(inner * KINDS, KINDS)

    def template_copy(i):
        return remote(
            msg, wbuf.at[slot], w_send.at[i], w_recv.at[q], (4 * i + m % SETS) * RING + dest_r, dest_q
        )

    def forward_copy(i):
        return remote(wbuf.at[mine], wbuf.at[mine], f_send.at[i], f_recv.at[inner], (4 * outer + i) * RING + r, q)

    def record_copy(i):
        return remote(record(i), xbuf.at[r], x_send.at[i], x_recv.at[r], group * RING + i, q)

    def halo_copy(i):
        return remote(record(i), xbuf.at[RING], h_send.at[i], x_recv.at[RING], (group - 1) * RING + i, q)

    def near_copy(i):
        return remote(
            all_ref.at[group], all_ref.at[group], s_send.at[i], s_recv.at[inner], (4 * outer + i) * RING + r, q
        )

    def far_copy(i):
        block = all_ref.at[pl.ds(4 * outer, 4)]
        return remote(block, block, g_send.at[i], g_recv.at[outer], (4 * i + inner) * RING + r, q)

    def part_copy(i):
        return remote(part.at[i], land.at[r], p_send.at[i], p_recv.at[r], group * RING + i, q)

    def half_copy(i):
        return remote(half, full.at[q], q_send.at[i], q_recv.at[q], m, i)

    away = [jnp.logical_not((i == outer) & lies_here) for i in range(4)]
    for i in range(4):
        pl.when(away[i])(lambda i=i: template_copy(i).start())

    @pl.when(lies_here)
    def _():
        wbuf[slot] = msg[...]

    each(RING, r, lambda i: record_copy(i).start())

    @pl.when(head)
    def _():
        for i in range(RING):
            halo_copy(i).start()

    for k in range(KINDS):
        here = (source == m) & (q == k)
        pl.when(jnp.logical_not(here))(
            lambda k=k: remote(msg, wbuf.at[inner * KINDS + k], w_send.at[0], w_recv.at[k], m, q).wait_recv()
        )
    each(4, inner, lambda i: forward_copy(i).start())

    local.wait()
    each(RING, r, lambda i: remote(record(0), xbuf.at[i], x_send.at[i], x_recv.at[i], m, q).wait_recv())

    @pl.when(group < GROUPS - 1)
    def _():
        remote(record(0), xbuf.at[RING], h_send.at[0], x_recv.at[RING], m, q).wait_recv()

    x = jnp.concatenate([xbuf[i].astype(f32) for i in range(RING + 1)], axis=1)
    all_ref[group] = block_sums(x, run_ref, sum_ref)
    each(4, inner, lambda i: near_copy(i).start())

    def forwarded(i):
        block = wbuf.at[pl.ds(i * KINDS, KINDS)]
        remote(block, block, f_send.at[i], f_recv.at[i], m, q).wait_recv()

    each(4, inner, forwarded)
    sel, weight = prepare(wbuf[...].astype(f32), a_ref)
    correlate(0, x, h_ref, a_ref, z_ref, corr_ref)

    def near(i):
        block = all_ref.at[4 * outer + i]
        remote(block, block, s_send.at[i], s_recv.at[i], m, q).wait_recv()

    each(4, inner, near)
    each(4, outer, lambda i: far_copy(i).start())
    for j in range(1, SETS):
        correlate(j, x, h_ref, a_ref, z_ref, corr_ref)

    def far(i):
        block = all_ref.at[pl.ds(4 * i, 4)]
        remote(block, block, g_send.at[i], g_recv.at[i], m, q).wait_recv()

    each(4, outer, far)
    energy = window_energy(group, all_ref, run_ref, sum_ref, chain_ref, outer_ref, edge_ref, part_ref)
    total = stacked(1.0 / jnp.sqrt(energy + EPS), weight, sel, corr_ref, n_ref, z_ref)
    for i in range(RING):
        part[i] = total[:, PIECE * i : PIECE * i + PIECE]

    each(RING, r, lambda i: part_copy(i).start())
    land[r] = part[r]
    each(RING, r, lambda i: remote(part.at[0], land.at[i], p_send.at[i], p_recv.at[i], m, q).wait_recv())
    half[...] = jnp.sum(land[...], axis=0)
    each(KINDS, q, lambda i: half_copy(i).start())
    full[q] = half[...]
    each(KINDS, q, lambda i: remote(half, full.at[i], q_send.at[i], q_recv.at[i], m, q).wait_recv())
    whole = jnp.sum(full[...], axis=0)
    row = lax.broadcasted_iota(jnp.int32, (8, PIECE), 0)
    out_ref[...] = jnp.sum(jnp.where(row == q, whole, 0.0), axis=0, keepdims=True)

    for i in range(4):
        pl.when(away[i])(lambda i=i: template_copy(i).wait_send())
    each(4, inner, lambda i: forward_copy(i).wait_send())
    each(RING, r, lambda i: record_copy(i).wait_send())

    @pl.when(head)
    def _():
        for i in range(RING):
            halo_copy(i).wait_send()

    each(4, inner, lambda i: near_copy(i).wait_send())
    each(4, outer, lambda i: far_copy(i).wait_send())
    each(RING, r, lambda i: part_copy(i).wait_send())
    each(KINDS, q, lambda i: half_copy(i).wait_send())


def local(records, templates, shifts, valid):
    vmem = pl.BlockSpec(memory_space=pltpu.VMEM)
    dma = pltpu.SemaphoreType.DMA
    return pl.pallas_call(
        kernel,
        out_shape=jax.ShapeDtypeStruct((1, PIECE), f32),
        in_specs=[pl.BlockSpec(memory_space=pl.ANY), vmem, vmem, vmem],
        out_specs=vmem,
        scratch_shapes=[
            pltpu.VMEM((RING + 1, ROWS, PIECE), bf16),
            pltpu.VMEM((SETS * KINDS, 16, 256), bf16),
            pltpu.VMEM((16, 256), bf16),
            pltpu.VMEM((GROUPS, 8, 128), f32),
            pltpu.VMEM((RING, 8, PIECE), f32),
            pltpu.VMEM((RING, 8, PIECE), f32),
            pltpu.VMEM((8, PIECE), f32),
            pltpu.VMEM((KINDS, 8, PIECE), f32),
            pltpu.VMEM((2, 256, NH), bf16),
            pltpu.VMEM((SETS, 128, BIG), bf16),
            pltpu.VMEM((2, 128, NZ), f32),
            pltpu.VMEM((256, NZ), bf16),
            pltpu.VMEM((128, NZ), f32),
            pltpu.VMEM((1280, 128), f32),
            pltpu.VMEM((128, 128), f32),
            pltpu.VMEM((256, 128), f32),
            pltpu.VMEM((256, 128), f32),
            pltpu.VMEM((256, 128), f32),
            pltpu.VMEM((128, 128), f32),
            dma((4,)), dma((KINDS,)),
            dma((4,)), dma((4,)),
            dma((RING,)), dma((RING + 1,)), dma((RING,)),
            dma((4,)), dma((4,)),
            dma((4,)), dma((4,)),
            dma((RING,)), dma((RING,)),
            dma((KINDS,)), dma((KINDS,)),
            dma,
        ],
        compiler_params=pltpu.CompilerParams(
            collective_id=0, has_side_effects=True, vmem_limit_bytes=40 * 1024 * 1024
        ),
    )(records, templates, shifts, valid)


def solution(mesh):
    in_specs = (P(None, "tm"), P("tmpl", "tm", None), P("tmpl", "tm"), P("tmpl", "tm"))
    return jax.shard_map(local, mesh=mesh, in_specs=in_specs, out_specs=P("tmpl", "tm"), check_vma=False)
```

```python
import functools

import jax
import jax.numpy as jnp
from jax import lax
from jax.experimental import pallas as pl
from jax.experimental.pallas import tpu as pltpu
from jax.sharding import PartitionSpec as P

L = 300
MAXS = 20
EPS = 1e-05
KINDS = 4
RING = 8
GROUPS = 16
COLUMN = 8
PIECE = 384
ROWS = 32
OCT = 8
SETS = ROWS // OCT
STEP = 32
SPAN = RING * PIECE
WIDE = SPAN + PIECE
NH = 3584
NZ = 3328
BIG = 3 * 256
QUARTER = SPAN // 4
LEVELS = 22
BLOCKS = (WIDE // 16)
CHAIN = 208

f32 = jnp.float32
bf16 = jnp.bfloat16


def prepare(message, a_ref):
    pairs = SETS * KINDS * OCT
    low = message[:, :OCT, :].reshape(pairs, 256)
    high = message[:, OCT:, :].reshape(pairs, 256)

    parts = [low[:, :128].astype(bf16), low[:, 128:].astype(bf16), high[:, :128].astype(bf16)]
    lane = lax.broadcasted_iota(jnp.int32, (128, 256), 1)
    line = lax.broadcasted_iota(jnp.int32, (128, 256), 0)
    same = (lane % OCT) == (line % OCT)
    for u_lo in range(4):
        spread = jnp.where(line == STEP * u_lo + lane // OCT, 1.0, 0.0).astype(bf16)
        for u_hi in range(3):
            wide = jnp.dot(parts[u_hi], spread, preferred_element_type=f32)
            block = jnp.where(same, wide, 0.0).astype(bf16)
            for j in range(SETS):
                a_ref[j, 32 * u_lo : 32 * u_lo + 32, 256 * u_hi : 256 * u_hi + 256] = block[32 * j : 32 * j + 32]

    shift = high[:, 128:129]
    valid = high[:, 129:130]
    column = lax.broadcasted_iota(jnp.int32, (pairs, 128), 1)
    squares = low[:, :128] ** 2 + low[:, 128:] ** 2 + high[:, :128] ** 2
    power = jnp.sum(squares, axis=1, keepdims=True) / L
    weight = valid / (L * jnp.sqrt(power + EPS))

    kind = (lax.broadcasted_iota(jnp.int32, (pairs, 128), 0) // OCT) % KINDS
    picked = (shift == (column // KINDS).astype(f32)) & (kind == column % KINDS)
    sel = jnp.transpose(jnp.where(picked, 1.0, 0.0)).astype(bf16)
    return jnp.concatenate([sel, sel], axis=1)[: 4 * LEVELS], weight


def shifted(j, x, h_ref):
    x8 = jnp.concatenate([x[OCT * j : OCT * j + OCT], jnp.zeros((OCT, NH - WIDE), f32)], axis=1)
    for i in range(STEP // 2):
        first = x8 if i == 0 else pltpu.roll(x8, NH - 2 * i, 1)
        second = pltpu.roll(x8, NH - 2 * i - 1, 1)
        h_ref[j, 16 * i : 16 * i + 16, :] = jnp.concatenate([first, second], axis=0).astype(bf16)


def correlate(j, h_ref, a_ref, z_ref, corr_ref):
    slot = j % 2
    for n in range(NZ // 256):
        acc = None
        for u_hi in range(3):
            part = jnp.dot(
                a_ref[j, :, 256 * u_hi : 256 * u_hi + 256],
                h_ref[j, :, 256 * n + 128 * u_hi : 256 * n + 128 * u_hi + 256],
                preferred_element_type=f32,
            )
            acc = part if acc is None else acc + part
        z_ref[slot, :, 256 * n : 256 * n + 256] = acc
    for k in range(KINDS):
        corr = z_ref[slot, 8 * k : 8 * k + 8, :]
        for u_lo in range(1, 4):
            corr = corr + pltpu.roll(z_ref[slot, 32 * u_lo + 8 * k : 32 * u_lo + 8 * k + 8, :], NZ - STEP * u_lo, 1)
        corr_ref[32 * j + 8 * k : 32 * j + 8 * k + 8, :] = corr


def running16(run_ref, start, rows, sum_ref):
    acc = run_ref[pl.ds(start, rows, stride=16), :]
    for d in range(1, 16):
        acc = acc + run_ref[pl.ds(start + d, rows, stride=16), :]
        run_ref[pl.ds(start + d, rows, stride=16), :] = acc
    sum_ref[:rows, :] = acc
    sum_ref[rows:, :] = jnp.zeros((128 - rows, 128), f32)
    outer = sum_ref[pl.ds(0, 8, stride=16), :]
    for c in range(1, 16):
        outer = outer + sum_ref[pl.ds(c, 8, stride=16), :]
        sum_ref[pl.ds(c, 8, stride=16), :] = outer
    return acc, outer


def block_sums(x, run_ref, sum_ref):
    squares = x * x
    stacked = jnp.concatenate([squares[:, QUARTER * s : QUARTER * s + QUARTER] for s in range(4)], axis=0)
    for i in range(QUARTER // 128):
        run_ref[128 * i : 128 * i + 128, :] = jnp.transpose(stacked[:, 128 * i : 128 * i + 128])
    acc, outer = running16(run_ref, 0, QUARTER // 16, sum_ref)
    final = acc[QUARTER // 16 - 1 : QUARTER // 16]
    before = sum_ref[QUARTER // 16 - 2 : QUARTER // 16 - 1, :]
    return jnp.concatenate([outer[:3], final, before, jnp.zeros((3, 128), f32)], axis=0)


def halo_sums(x, run_ref, tail_ref):
    halo = jnp.concatenate([x * x, jnp.zeros((128 - ROWS, PIECE), f32)], axis=0)
    for i in range(PIECE // 128):
        run_ref[QUARTER + 128 * i : QUARTER + 128 * i + 128, :] = jnp.transpose(halo[:, 128 * i : 128 * i + 128])
    running16(run_ref, QUARTER, PIECE // 16, tail_ref)


def window_energy(group, all_ref, run_ref, sum_ref, tail_ref, chain_ref, outer_ref, edge_ref, part_ref):
    for g in range(GROUPS):
        totals = all_ref[g]
        for s in range(4):
            moved = totals if s == 0 else pltpu.roll(totals, 128 - ROWS * s, 1)
            chain_ref[12 * g + 3 * s : 12 * g + 3 * s + 3, :] = moved[:3]
    chain_ref[12 * GROUPS :, :] = jnp.zeros((256 - 12 * GROUPS, 128), f32)
    plain = chain_ref[:CHAIN, :]
    acc = chain_ref[pl.ds(0, 16, stride=16), :]
    for b in range(1, 16):
        acc = acc + chain_ref[pl.ds(b, 16, stride=16), :]
        chain_ref[pl.ds(b, 16, stride=16), :] = acc
    outer_ref[:8, :] = jnp.zeros((8, 128), f32)
    top = jnp.zeros((1, 128), f32)
    for a in range(CHAIN // 16):
        outer_ref[16 * a + 9 : 16 * a + 25, :] = chain_ref[16 * a : 16 * a + 16, :] + top
        top = top + acc[a : a + 1]
    outer_ref[8:9, :] = jnp.zeros((1, 128), f32)
    edge_ref[:8, :] = jnp.zeros((8, 128), f32)
    edge_ref[9 : 9 + CHAIN, :] = plain + outer_ref[8 : 8 + CHAIN, :]
    edge_ref[8:9, :] = jnp.zeros((1, 128), f32)
    mine = outer_ref[7:23, :]
    edge = edge_ref[7:23, :]
    for g in range(1, GROUPS):
        here = group == g
        mine = jnp.where(here, outer_ref[12 * g + 7 : 12 * g + 23, :], mine)
        edge = jnp.where(here, edge_ref[12 * g + 7 : 12 * g + 23, :], edge)
    lane = lax.broadcasted_iota(jnp.int32, (1, 128), 1) // ROWS

    def spread(rows, b):
        out = rows[1 + b : 2 + b]
        for s in range(1, 4):
            out = jnp.where(lane == s, pltpu.roll(rows[1 + 3 * s + b : 2 + 3 * s + b], ROWS * s, 1), out)
        return out

    befores = [spread(mine, b) for b in range(3)] + [mine[13:14], mine[14:15]]
    edges = [spread(edge, b) for b in range(3)] + [edge[13:14], edge[14:15]]
    for b in range(5):
        sums = sum_ref[16 * b : 16 * b + 16, :] if b < 3 else tail_ref[16 * b - 48 : 16 * b - 32, :]
        part_ref[16 * b + 1 : 16 * b + 17, :] = sums + befores[b]
        part_ref[16 * b : 16 * b + 1, :] = edges[b]
    quarter = QUARTER
    rows = (quarter + PIECE) // 16
    base = part_ref[:rows, :]
    for d in range(16):
        run_ref[pl.ds(d, rows, stride=16), :] = run_ref[pl.ds(d, rows, stride=16), :] + base
    ahead = pltpu.roll(all_ref[jnp.maximum(group - 1, 0)], ROWS, 1)
    last = jnp.where(group > 0, ahead[3:4] + (ahead[4:5] + mine[0:1]), 0.0)
    stretch = quarter + PIECE
    run_ref[stretch : stretch + 128, :] = jnp.concatenate([jnp.zeros((127, 128), f32), last], axis=0)
    main = jnp.concatenate(
        [jnp.transpose(run_ref[128 * i : 128 * i + 128, :]) for i in range(quarter // 128)], axis=1
    )
    tail = [jnp.transpose(run_ref[quarter + 128 * i : quarter + 128 * i + 128, :])[:ROWS] for i in range(4)]
    running = jnp.concatenate([main[ROWS * s : ROWS * s + ROWS] for s in range(4)] + tail, axis=1)
    energy = pltpu.roll(running, NH - (L - 1), 1) - pltpu.roll(running, 1, 1)
    return jnp.maximum(energy, 0.0)[:, :NZ] / L


def stacked(inverse, weight, sel, corr_ref, n_ref, z_ref):
    pairs = SETS * KINDS * OCT
    for j in range(SETS):
        for k in range(KINDS):
            row = 32 * j + 8 * k
            corr_ref[row : row + 8, :] = corr_ref[row : row + 8, :] * inverse[OCT * j : OCT * j + OCT] * weight[row : row + 8]
        normed = corr_ref[32 * j : 32 * j + 32, :]
        head = normed.astype(bf16)
        n_ref[32 * j : 32 * j + 32, :] = head
        n_ref[pairs + 32 * j : pairs + 32 * j + 32, :] = (normed - head.astype(f32)).astype(bf16)
    for n in range(NZ // 256):
        z_ref[0, : 4 * LEVELS, 256 * n : 256 * n + 256] = jnp.dot(
            sel, n_ref[:, 256 * n : 256 * n + 256], preferred_element_type=f32
        )
    total = z_ref[0, :8, :]
    for i in range(1, LEVELS // 2):
        total = total + pltpu.roll(z_ref[0, 8 * i : 8 * i + 8, :], NZ - 2 * i, 1)
    return total + pltpu.roll(pltpu.roll(total, NZ - 1, 1), 4, 0)


def kernel(
    rec_ref, tmpl_ref, shift_ref, valid_ref, out_ref,
    xbuf, wbuf, ybuf, msg, all_ref, part, land, half, full, tbuf, ibuf,
    h_ref, a_ref, z_ref, n_ref, corr_ref, run_ref, sum_ref, tail_ref, chain_ref, outer_ref, edge_ref, part_ref,
    w_send, w_recv, f_send, f_recv, x_send, x_recv, h_send, s_send, s_recv, g_send, g_recv,
    p_send, p_recv, q_send, q_recv, own,
):
    m, q = lax.axis_index("tm"), lax.axis_index("tmpl")
    group, r = m // RING, m % RING
    high, y = group // COLUMN, group % COLUMN
    x_at, core = r // 2, r % 2
    p = 2 * q + core
    to_self = p // 4 == high
    barrier = pltpu.get_barrier_semaphore()

    def signal(tm, tmpl):
        pl.semaphore_signal(barrier, inc=1, device_id=(tm, tmpl), device_id_type=pl.DeviceIdType.MESH)

    def remote(src, dst, send, recv, tm, tmpl):
        return pltpu.make_async_remote_copy(
            src_ref=src, dst_ref=dst, send_sem=send, recv_sem=recv,
            device_id=(tm, tmpl), device_id_type=pl.DeviceIdType.MESH,
        )

    def each(count, skip, step):
        for i in range(count):
            pl.when(i != skip)(functools.partial(step, i))

    def at_y(i):
        return (high * COLUMN + i) * RING + r

    local = [
        pltpu.make_async_copy(tmpl_ref, tbuf, own.at[0]),
        pltpu.make_async_copy(shift_ref, ibuf.at[0], own.at[1]),
        pltpu.make_async_copy(valid_ref, ibuf.at[1], own.at[2]),
        pltpu.make_async_copy(rec_ref.at[pl.ds(2 * p, 2), x_at], xbuf.at[r], own.at[3]),
    ]
    for copy in local:
        copy.start()

    other = (1 - high) * COLUMN * RING + y * RING + r
    signal(other, q)
    each(COLUMN, y, lambda i: signal(at_y(i), q))
    comes = [
        [jnp.logical_not(to_self & (core == cs) & (q == k)) for k in range(KINDS)] for cs in range(2)
    ]
    for cs in range(2):
        for k in range(KINDS):
            source = ((p // 4) * COLUMN + y) * RING + 2 * x_at + cs
            pl.when(comes[cs][k])(functools.partial(signal, source, k))
    each(RING, r, lambda i: signal(group * RING + i, q))
    each(KINDS, q, lambda i: signal(m, i))

    @pl.when(group < GROUPS - 1)
    def _():
        signal(m + RING, q)

    for copy in local:
        copy.wait()

    waves = tbuf[0].astype(f32)
    eye = lax.broadcasted_iota(jnp.int32, (OCT, OCT), 0) == lax.broadcasted_iota(jnp.int32, (OCT, OCT), 1)
    moves = jnp.sum(jnp.where(eye, ibuf[0].astype(f32), 0.0), axis=1, keepdims=True)
    masks = jnp.sum(jnp.where(eye, ibuf[1].astype(f32), 0.0), axis=1, keepdims=True)
    lane = lax.broadcasted_iota(jnp.int32, (OCT, 128), 1)
    extra = jnp.where(lane == 0, moves, jnp.where(lane == 1, masks, 0.0))
    tail = jnp.concatenate([waves[:, 256:], jnp.zeros((OCT, 128 - (L - 256)), f32)], axis=1)
    msg[...] = jnp.concatenate([waves[:, :256], jnp.concatenate([tail, extra], axis=1)], axis=0).astype(bf16)

    @pl.when(group == GROUPS - 1)
    def _():
        xbuf[RING] = jnp.zeros((2, ROWS // 2, PIECE), bf16)

    count = (
        1 + (COLUMN - 1) + 8 - to_self.astype(jnp.int32)
        + (RING - 1) + (KINDS - 1) + (group > 0).astype(jnp.int32)
    )
    pl.semaphore_wait(barrier, count)

    def record(i):
        return rec_ref.at[pl.ds(2 * (2 * q + i % 2), 2), i // 2]

    def template_copy(i):
        return remote(msg, ybuf.at[y], w_send.at[i], w_recv.at[y], at_y(i), q)

    def pair_copy(i, z):
        tm = (z * COLUMN + y) * RING + 2 * x_at + i % 2
        return remote(
            ybuf.at[pl.ds(2 * i, 2)], wbuf.at[KINDS * core + q], f_send.at[2 * i + z], f_recv.at[KINDS * core + q],
            tm, 2 * high + i // 2,
        )

    def record_copy(i):
        return remote(record(i), xbuf.at[r], x_send.at[i], x_recv.at[r], group * RING + i, q)

    def halo_copy():
        return remote(xbuf.at[0], xbuf.at[RING], h_send, x_recv.at[RING], m - RING, q)

    def near_copy(i):
        return remote(all_ref.at[group], all_ref.at[group], s_send.at[i], s_recv.at[y], at_y(i), q)

    def far_copy():
        block = all_ref.at[pl.ds(COLUMN * high, COLUMN)]
        return remote(block, block, g_send, g_recv, other, q)

    def part_copy(i):
        return remote(
            part.at[i, pl.ds(0, KINDS)], land.at[r, pl.ds(0, KINDS)], p_send.at[i], p_recv.at[r], group * RING + i, q
        )

    def half_copy(i):
        return remote(half, full.at[q], q_send.at[i], q_recv.at[q], m, i)

    goes = [[jnp.logical_not(to_self & (p % 4 == i) & (high == z)) for z in range(2)] for i in range(4)]

    each(RING, r, lambda i: record_copy(i).start())
    each(COLUMN, y, lambda i: template_copy(i).start())
    ybuf[y] = msg[...]
    each(RING, r, lambda i: remote(xbuf.at[i], xbuf.at[i], x_send.at[i], x_recv.at[i], m, q).wait_recv())

    @pl.when(group > 0)
    def _():
        halo_copy().start()

    main = jnp.concatenate([xbuf[i].astype(f32).reshape(ROWS, PIECE) for i in range(RING)], axis=1)
    all_ref[group] = block_sums(main, run_ref, sum_ref)
    each(COLUMN, y, lambda i: near_copy(i).start())

    each(COLUMN, y, lambda i: remote(msg, ybuf.at[i], w_send.at[i], w_recv.at[i], m, q).wait_recv())
    for i in range(4):
        for z in range(2):
            pl.when(goes[i][z])(lambda i=i, z=z: pair_copy(i, z).start())

    @pl.when(to_self)
    def _():
        wbuf[KINDS * core + q] = ybuf[pl.ds(2 * (p % 4), 2)]

    @pl.when(group < GROUPS - 1)
    def _():
        remote(xbuf.at[0], xbuf.at[RING], h_send, x_recv.at[RING], m, q).wait_recv()

    halo = xbuf[RING].astype(f32).reshape(ROWS, PIECE)
    halo_sums(halo, run_ref, tail_ref)
    x = jnp.concatenate([main, halo], axis=1)
    for j in range(SETS):
        shifted(j, x, h_ref)

    def near(i):
        block = all_ref.at[high * COLUMN + i]
        remote(block, block, s_send.at[i], s_recv.at[i], m, q).wait_recv()

    each(COLUMN, y, near)
    far_copy().start()

    for cs in range(2):
        for k in range(KINDS):
            slot = KINDS * cs + k
            pl.when(comes[cs][k])(
                lambda slot=slot: remote(
                    wbuf.at[slot], wbuf.at[slot], f_send.at[0], f_recv.at[slot], m, q
                ).wait_recv()
            )
    shards = wbuf[...].astype(f32)
    shards = [shards[KINDS * cs + k, e : e + 1] for e in range(2) for cs in range(2) for k in range(KINDS)]
    sel, weight = prepare(jnp.concatenate(shards, axis=0), a_ref)
    for j in range(SETS):
        correlate(j, h_ref, a_ref, z_ref, corr_ref)

    far = all_ref.at[pl.ds(COLUMN * (1 - high), COLUMN)]
    remote(far, far, g_send, g_recv, m, q).wait_recv()
    energy = window_energy(group, all_ref, run_ref, sum_ref, tail_ref, chain_ref, outer_ref, edge_ref, part_ref)
    total = stacked(1.0 / jnp.sqrt(energy + EPS), weight, sel, corr_ref, n_ref, z_ref)
    for i in range(RING):
        part[i] = total[:, PIECE * i : PIECE * i + PIECE]

    each(RING, r, lambda i: part_copy(i).start())
    land[r, :KINDS] = part[r, :KINDS]
    each(
        RING, r,
        lambda i: remote(
            part.at[0, pl.ds(0, KINDS)], land.at[i, pl.ds(0, KINDS)], p_send.at[i], p_recv.at[i], m, q
        ).wait_recv(),
    )
    half[...] = jnp.concatenate([jnp.sum(land[:, :KINDS], axis=0), jnp.zeros((KINDS, PIECE), f32)], axis=0)
    each(KINDS, q, lambda i: half_copy(i).start())
    full[q] = half[...]
    each(KINDS, q, lambda i: remote(half, full.at[i], q_send.at[i], q_recv.at[i], m, q).wait_recv())
    whole = jnp.sum(full[...], axis=0)
    row = lax.broadcasted_iota(jnp.int32, (8, PIECE), 0)
    out_ref[...] = jnp.sum(jnp.where(row == q, whole, 0.0), axis=0, keepdims=True)

    each(COLUMN, y, lambda i: template_copy(i).wait_send())
    each(RING, r, lambda i: record_copy(i).wait_send())

    @pl.when(group > 0)
    def _():
        halo_copy().wait_send()

    for i in range(4):
        for z in range(2):
            pl.when(goes[i][z])(lambda i=i, z=z: pair_copy(i, z).wait_send())
    each(COLUMN, y, lambda i: near_copy(i).wait_send())
    far_copy().wait_send()
    each(RING, r, lambda i: part_copy(i).wait_send())
    each(KINDS, q, lambda i: half_copy(i).wait_send())


def local(records, templates, shifts, valid):
    hbm = pl.BlockSpec(memory_space=pltpu.HBM)
    dma = pltpu.SemaphoreType.DMA
    return pl.pallas_call(
        kernel,
        out_shape=jax.ShapeDtypeStruct((1, PIECE), f32),
        in_specs=[hbm] * 4,
        out_specs=pl.BlockSpec(memory_space=pltpu.VMEM),
        scratch_shapes=[
            pltpu.VMEM((RING + 1, 2, ROWS // 2, PIECE), bf16),
            pltpu.VMEM((2 * KINDS, 2, 16, 256), bf16),
            pltpu.VMEM((COLUMN, 16, 256), bf16),
            pltpu.VMEM((16, 256), bf16),
            pltpu.VMEM((GROUPS, 8, 128), f32),
            pltpu.VMEM((RING, 8, PIECE), f32),
            pltpu.VMEM((RING, 8, PIECE), f32),
            pltpu.VMEM((8, PIECE), f32),
            pltpu.VMEM((KINDS, 8, PIECE), f32),
            pltpu.VMEM((1, OCT, L), bf16),
            pltpu.VMEM((2, 1, OCT), jnp.int32),
            pltpu.VMEM((SETS, 256, NH), bf16),
            pltpu.VMEM((SETS, 128, BIG), bf16),
            pltpu.VMEM((2, 128, NZ), f32),
            pltpu.VMEM((256, NZ), bf16),
            pltpu.VMEM((128, NZ), f32),
            pltpu.VMEM((1280, 128), f32),
            pltpu.VMEM((128, 128), f32),
            pltpu.VMEM((128, 128), f32),
            pltpu.VMEM((256, 128), f32),
            pltpu.VMEM((256, 128), f32),
            pltpu.VMEM((256, 128), f32),
            pltpu.VMEM((128, 128), f32),
            dma((COLUMN,)), dma((COLUMN,)),
            dma((8,)), dma((2 * KINDS,)),
            dma((RING,)), dma((RING + 1,)), dma,
            dma((COLUMN,)), dma((COLUMN,)),
            dma, dma,
            dma((RING,)), dma((RING,)),
            dma((KINDS,)), dma((KINDS,)),
            dma((4,)),
        ],
        compiler_params=pltpu.CompilerParams(
            collective_id=0, has_side_effects=True, vmem_limit_bytes=63 * 1024 * 1024
        ),
    )(records.reshape(GROUPS, 4, 16, PIECE), templates, shifts, valid)


def solution(mesh):
    in_specs = (P(None, "tm"), P("tmpl", "tm", None), P("tmpl", "tm"), P("tmpl", "tm"))
    return jax.shard_map(local, mesh=mesh, in_specs=in_specs, out_specs=P("tmpl", "tm"), check_vma=False)
```

```python
import functools

import jax
import jax.numpy as jnp
from jax import lax
from jax.experimental import pallas as pl
from jax.experimental.pallas import tpu as pltpu
from jax.sharding import PartitionSpec as P

L = 300
MAXS = 20
EPS = 1e-05
KINDS = 4
RING = 8
GROUPS = 16
COLUMN = 8
PIECE = 384
ROWS = 32
OCT = 8
SETS = ROWS // OCT
STEP = 32
SPAN = RING * PIECE
WIDE = SPAN + PIECE
NH = 3584
NZ = 3328
BIG = 3 * 256
QUARTER = SPAN // 4
LEVELS = 22
BLOCKS = (WIDE // 16)
CHAIN = 208

f32 = jnp.float32
bf16 = jnp.bfloat16


def prepare(message, a_ref):
    pairs = SETS * KINDS * OCT
    low = message[:, :OCT, :].reshape(pairs, 256)
    high = message[:, OCT:, :].reshape(pairs, 256)

    parts = [low[:, :128].astype(bf16), low[:, 128:].astype(bf16), high[:, :128].astype(bf16)]
    lane = lax.broadcasted_iota(jnp.int32, (128, 256), 1)
    line = lax.broadcasted_iota(jnp.int32, (128, 256), 0)
    same = (lane % OCT) == (line % OCT)
    for u_lo in range(4):
        spread = jnp.where(line == STEP * u_lo + lane // OCT, 1.0, 0.0).astype(bf16)
        for u_hi in range(3):
            wide = jnp.dot(parts[u_hi], spread, preferred_element_type=f32)
            block = jnp.where(same, wide, 0.0).astype(bf16)
            for j in range(SETS):
                a_ref[j, 32 * u_lo : 32 * u_lo + 32, 256 * u_hi : 256 * u_hi + 256] = block[32 * j : 32 * j + 32]

    shift = high[:, 128:129]
    valid = high[:, 129:130]
    column = lax.broadcasted_iota(jnp.int32, (pairs, 128), 1)
    squares = low[:, :128] ** 2 + low[:, 128:] ** 2 + high[:, :128] ** 2
    power = jnp.sum(squares, axis=1, keepdims=True) / L
    weight = valid / (L * jnp.sqrt(power + EPS))

    kind = (lax.broadcasted_iota(jnp.int32, (pairs, 128), 0) // OCT) % KINDS
    picked = (shift == (column // KINDS).astype(f32)) & (kind == column % KINDS)
    sel = jnp.transpose(jnp.where(picked, 1.0, 0.0)).astype(bf16)
    return jnp.concatenate([sel, sel], axis=1)[: 4 * LEVELS], weight


def shifted(j, x, h_ref):
    x8 = jnp.concatenate([x[OCT * j : OCT * j + OCT], jnp.zeros((OCT, NH - WIDE), f32)], axis=1)
    for i in range(STEP // 2):
        first = x8 if i == 0 else pltpu.roll(x8, NH - 2 * i, 1)
        second = pltpu.roll(x8, NH - 2 * i - 1, 1)
        h_ref[j, 16 * i : 16 * i + 16, :] = jnp.concatenate([first, second], axis=0).astype(bf16)


def correlate(j, h_ref, a_ref, z_ref, corr_ref):
    slot = j % 2
    for n in range(NZ // 256):
        acc = None
        for u_hi in range(3):
            rows = 64 if u_hi == 2 else 128
            part = jnp.dot(
                a_ref[j, :rows, 256 * u_hi : 256 * u_hi + 256],
                h_ref[j, :, 256 * n + 128 * u_hi : 256 * n + 128 * u_hi + 256],
                preferred_element_type=f32,
            )
            acc = part if acc is None else jnp.concatenate([acc[:rows] + part, acc[rows:]], axis=0) if rows < 128 else acc + part
        z_ref[slot, :, 256 * n : 256 * n + 256] = acc
    for k in range(KINDS):
        corr = z_ref[slot, 8 * k : 8 * k + 8, :]
        for u_lo in range(1, 4):
            corr = corr + pltpu.roll(z_ref[slot, 32 * u_lo + 8 * k : 32 * u_lo + 8 * k + 8, :], NZ - STEP * u_lo, 1)
        corr_ref[32 * j + 8 * k : 32 * j + 8 * k + 8, :] = corr


def running16(run_ref, start, rows, sum_ref):
    acc = run_ref[pl.ds(start, rows, stride=16), :]
    for d in range(1, 16):
        acc = acc + run_ref[pl.ds(start + d, rows, stride=16), :]
        run_ref[pl.ds(start + d, rows, stride=16), :] = acc
    sum_ref[:rows, :] = acc
    sum_ref[rows:, :] = jnp.zeros((128 - rows, 128), f32)
    outer = sum_ref[pl.ds(0, 8, stride=16), :]
    for c in range(1, 16):
        outer = outer + sum_ref[pl.ds(c, 8, stride=16), :]
        sum_ref[pl.ds(c, 8, stride=16), :] = outer
    return acc, outer


def block_sums(x, run_ref, sum_ref):
    squares = x * x
    stacked = jnp.concatenate([squares[:, QUARTER * s : QUARTER * s + QUARTER] for s in range(4)], axis=0)
    for i in range(QUARTER // 128):
        run_ref[128 * i : 128 * i + 128, :] = jnp.transpose(stacked[:, 128 * i : 128 * i + 128])
    acc, outer = running16(run_ref, 0, QUARTER // 16, sum_ref)
    final = acc[QUARTER // 16 - 1 : QUARTER // 16]
    before = sum_ref[QUARTER // 16 - 2 : QUARTER // 16 - 1, :]
    return jnp.concatenate([outer[:3], final, before, jnp.zeros((3, 128), f32)], axis=0)


def halo_sums(x, run_ref, tail_ref):
    halo = jnp.concatenate([x * x, jnp.zeros((128 - ROWS, PIECE), f32)], axis=0)
    for i in range(PIECE // 128):
        run_ref[QUARTER + 128 * i : QUARTER + 128 * i + 128, :] = jnp.transpose(halo[:, 128 * i : 128 * i + 128])
    _, outer = running16(run_ref, QUARTER, PIECE // 16, tail_ref)
    return outer[:1]


def window_energy(group, all_ref, run_ref, sum_ref, tail_ref, chain_ref, outer_ref, edge_ref, part_ref):
    for g in range(GROUPS):
        totals = all_ref[g]
        for s in range(4):
            moved = totals if s == 0 else pltpu.roll(totals, 128 - ROWS * s, 1)
            chain_ref[12 * g + 3 * s : 12 * g + 3 * s + 3, :] = moved[:3]
    chain_ref[12 * GROUPS :, :] = jnp.zeros((256 - 12 * GROUPS, 128), f32)
    plain = chain_ref[:CHAIN, :]
    acc = chain_ref[pl.ds(0, 16, stride=16), :]
    for b in range(1, 16):
        acc = acc + chain_ref[pl.ds(b, 16, stride=16), :]
        chain_ref[pl.ds(b, 16, stride=16), :] = acc
    outer_ref[:8, :] = jnp.zeros((8, 128), f32)
    top = jnp.zeros((1, 128), f32)
    for a in range(CHAIN // 16):
        outer_ref[16 * a + 9 : 16 * a + 25, :] = chain_ref[16 * a : 16 * a + 16, :] + top
        top = top + acc[a : a + 1]
    outer_ref[8:9, :] = jnp.zeros((1, 128), f32)
    edge_ref[:8, :] = jnp.zeros((8, 128), f32)
    edge_ref[9 : 9 + CHAIN, :] = plain + outer_ref[8 : 8 + CHAIN, :]
    edge_ref[8:9, :] = jnp.zeros((1, 128), f32)
    mine = outer_ref[7:23, :]
    edge = edge_ref[7:23, :]
    for g in range(1, GROUPS):
        here = group == g
        mine = jnp.where(here, outer_ref[12 * g + 7 : 12 * g + 23, :], mine)
        edge = jnp.where(here, edge_ref[12 * g + 7 : 12 * g + 23, :], edge)
    lane = lax.broadcasted_iota(jnp.int32, (1, 128), 1) // ROWS

    def spread(rows, b):
        out = rows[1 + b : 2 + b]
        for s in range(1, 4):
            out = jnp.where(lane == s, pltpu.roll(rows[1 + 3 * s + b : 2 + 3 * s + b], ROWS * s, 1), out)
        return out

    befores = [spread(mine, b) for b in range(3)] + [mine[13:14], mine[14:15]]
    edges = [spread(edge, b) for b in range(3)] + [edge[13:14], edge[14:15]]
    for b in range(5):
        sums = sum_ref[16 * b : 16 * b + 16, :] if b < 3 else tail_ref[16 * b - 48 : 16 * b - 32, :]
        part_ref[16 * b + 1 : 16 * b + 17, :] = sums + befores[b]
        part_ref[16 * b : 16 * b + 1, :] = edges[b]
    quarter = QUARTER
    rows = (quarter + PIECE) // 16
    base = part_ref[:rows, :]
    for d in range(16):
        run_ref[pl.ds(d, rows, stride=16), :] = run_ref[pl.ds(d, rows, stride=16), :] + base
    ahead = pltpu.roll(all_ref[jnp.maximum(group - 1, 0)], ROWS, 1)
    last = jnp.where(group > 0, ahead[3:4] + (ahead[4:5] + mine[0:1]), 0.0)
    stretch = quarter + PIECE
    run_ref[stretch : stretch + 128, :] = jnp.concatenate([jnp.zeros((127, 128), f32), last], axis=0)
    main = jnp.concatenate(
        [jnp.transpose(run_ref[128 * i : 128 * i + 128, :]) for i in range(quarter // 128)], axis=1
    )
    tail = [jnp.transpose(run_ref[quarter + 128 * i : quarter + 128 * i + 128, :])[:ROWS] for i in range(4)]
    running = jnp.concatenate([main[ROWS * s : ROWS * s + ROWS] for s in range(4)] + tail, axis=1)
    energy = pltpu.roll(running, NH - (L - 1), 1) - pltpu.roll(running, 1, 1)
    return jnp.maximum(energy, 0.0)[:, :NZ] / L


def stacked(inverse, weight, sel, corr_ref, n_ref, z_ref):
    pairs = SETS * KINDS * OCT
    for j in range(SETS):
        for k in range(KINDS):
            row = 32 * j + 8 * k
            corr_ref[row : row + 8, :] = corr_ref[row : row + 8, :] * inverse[OCT * j : OCT * j + OCT] * weight[row : row + 8]
        normed = corr_ref[32 * j : 32 * j + 32, :]
        head = normed.astype(bf16)
        n_ref[32 * j : 32 * j + 32, :] = head
        n_ref[pairs + 32 * j : pairs + 32 * j + 32, :] = (normed - head.astype(f32)).astype(bf16)
    for n in range(NZ // 256):
        z_ref[0, : 4 * LEVELS, 256 * n : 256 * n + 256] = jnp.dot(
            sel, n_ref[:, 256 * n : 256 * n + 256], preferred_element_type=f32
        )
    total = z_ref[0, :8, :]
    for i in range(1, LEVELS // 2):
        total = total + pltpu.roll(z_ref[0, 8 * i : 8 * i + 8, :], NZ - 2 * i, 1)
    return total + pltpu.roll(pltpu.roll(total, NZ - 1, 1), 4, 0)


def kernel(
    rec_ref, tmpl_ref, shift_ref, valid_ref, out_ref,
    xbuf, wbuf, ybuf, msg, all_ref, part, land, tbuf, ibuf,
    h_ref, a_ref, z_ref, n_ref, corr_ref, run_ref, sum_ref, tail_ref, chain_ref, outer_ref, edge_ref, part_ref, root_ref,
    w_send, w_recv, f_send, f_recv, x_send, x_recv, h_send, s_send, s_recv, g_send, g_recv,
    p_send, p_recv, own, ready,
):
    m, q = lax.axis_index("tm"), lax.axis_index("tmpl")
    group, r = m // RING, m % RING
    high, y = group // COLUMN, group % COLUMN
    x_at, core = r // 2, r % 2
    p = 2 * q + core
    to_self = p // 4 == high
    barrier = pltpu.get_barrier_semaphore()

    def signal(tm, tmpl):
        pl.semaphore_signal(barrier, inc=1, device_id=(tm, tmpl), device_id_type=pl.DeviceIdType.MESH)

    def remote(src, dst, send, recv, tm, tmpl):
        return pltpu.make_async_remote_copy(
            src_ref=src, dst_ref=dst, send_sem=send, recv_sem=recv,
            device_id=(tm, tmpl), device_id_type=pl.DeviceIdType.MESH,
        )

    def each(count, skip, step):
        for i in range(count):
            pl.when(i != skip)(functools.partial(step, i))

    def at_y(i):
        return (high * COLUMN + i) * RING + r

    local = [
        pltpu.make_async_copy(tmpl_ref, tbuf, own.at[0]),
        pltpu.make_async_copy(shift_ref, ibuf.at[0], own.at[1]),
        pltpu.make_async_copy(valid_ref, ibuf.at[1], own.at[2]),
        pltpu.make_async_copy(rec_ref.at[pl.ds(2 * p, 2), x_at], xbuf.at[r], own.at[3]),
    ]
    for copy in local:
        copy.start()

    low = high == 0
    other = (1 - high) * COLUMN * RING + y * RING + r

    def pair_target(i, z):
        return (z * COLUMN + y) * RING + 2 * x_at + i % 2, 2 * high + i // 2

    @pl.when(low)
    def _():
        signal(other, q)
        for i in range(4):
            signal(*pair_target(i, 1))

    each(COLUMN, y, lambda i: signal(at_y(i), q))
    comes = [
        [jnp.logical_not(to_self & (core == cs) & (q == k)) for k in range(KINDS)] for cs in range(2)
    ]
    for cs in range(2):
        for k in range(KINDS):
            source = ((p // 4) * COLUMN + y) * RING + 2 * x_at + cs
            pl.when(comes[cs][k] & (low | to_self))(functools.partial(signal, source, k))
    each(RING * KINDS, KINDS * r + q, lambda i: signal(group * RING + i // KINDS, i % KINDS))

    @pl.when(group < GROUPS - 1)
    def _():
        signal(m + RING, q)

    @pl.when(group == GROUPS - 1)
    def _():
        xbuf[RING] = jnp.zeros((2, ROWS // 2, PIECE), bf16)

    count = (
        (COLUMN - 1) + 4 - to_self.astype(jnp.int32)
        + (RING * KINDS - 1) + (group > 0).astype(jnp.int32)
        + high * (5 + 8 * (1 - to_self.astype(jnp.int32)))
    )

    @pl.when(low)
    def _():
        all_ref[COLUMN:] = jnp.zeros((COLUMN, 8, 128), f32)

    pl.semaphore_wait(barrier, count)

    def answer(tm, tmpl):
        pl.semaphore_signal(ready, inc=1, device_id=(tm, tmpl), device_id_type=pl.DeviceIdType.MESH)

    @pl.when(high == 1)
    def _():
        answer(other, q)

    @pl.when((high == 1) & jnp.logical_not(to_self))
    def _():
        for cs in range(2):
            for k in range(KINDS):
                answer(y * RING + 2 * x_at + cs, k)

    def record(i):
        return rec_ref.at[pl.ds(2 * (2 * q + i % 2), 2), i // 2]

    def template_copy(i):
        return remote(msg, ybuf.at[y], w_send.at[i], w_recv.at[y], at_y(i), q)

    def pair_copy(i, z):
        return remote(
            ybuf.at[pl.ds(2 * i, 2)], wbuf.at[KINDS * core + q], f_send.at[2 * i + z], f_recv.at[KINDS * core + q],
            *pair_target(i, z),
        )

    def record_copy(i):
        return remote(record(i), xbuf.at[r], x_send.at[i], x_recv.at[r], group * RING + i, q)

    def halo_copy():
        return remote(xbuf.at[0], xbuf.at[RING], h_send, x_recv.at[RING], m - RING, q)

    def near_copy(i):
        return remote(all_ref.at[group], all_ref.at[group], s_send.at[i], s_recv.at[y], at_y(i), q)

    def far_copy():
        block = all_ref.at[pl.ds(COLUMN * high, COLUMN)]
        return remote(block, block, g_send, g_recv, other, q)

    def part_copy(i):
        me = KINDS * r + q
        return remote(part.at[i], land.at[me], p_send.at[i], p_recv.at[me], group * RING + i // KINDS, i % KINDS)

    goes = [[jnp.logical_not(to_self & (p % 4 == i) & (high == z)) for z in range(2)] for i in range(4)]

    each(RING, r, lambda i: record_copy(i).start())
    for copy in local[:3]:
        copy.wait()

    waves = tbuf[0].astype(f32)
    eye = lax.broadcasted_iota(jnp.int32, (OCT, OCT), 0) == lax.broadcasted_iota(jnp.int32, (OCT, OCT), 1)
    moves = jnp.sum(jnp.where(eye, ibuf[0].astype(f32), 0.0), axis=1, keepdims=True)
    masks = jnp.sum(jnp.where(eye, ibuf[1].astype(f32), 0.0), axis=1, keepdims=True)
    lane = lax.broadcasted_iota(jnp.int32, (OCT, 128), 1)
    extra = jnp.where(lane == 0, moves, jnp.where(lane == 1, masks, 0.0))
    tail = jnp.concatenate([waves[:, 256:], jnp.zeros((OCT, 128 - (L - 256)), f32)], axis=1)
    msg[...] = jnp.concatenate([waves[:, :256], jnp.concatenate([tail, extra], axis=1)], axis=0).astype(bf16)

    each(COLUMN, y, lambda i: template_copy(i).start())
    ybuf[y] = msg[...]
    local[3].wait()
    each(RING, r, lambda i: remote(xbuf.at[i], xbuf.at[i], x_send.at[i], x_recv.at[i], m, q).wait_recv())

    @pl.when(group > 0)
    def _():
        halo_copy().start()

    main = jnp.concatenate([xbuf[i].astype(f32).reshape(ROWS, PIECE) for i in range(RING)], axis=1)
    all_ref[group] = block_sums(main, run_ref, sum_ref)
    each(COLUMN, y, lambda i: near_copy(i).start())

    each(COLUMN, y, lambda i: remote(msg, ybuf.at[i], w_send.at[i], w_recv.at[i], m, q).wait_recv())
    for z in range(2):
        for i in range(4):
            pl.when(goes[i][z] & (high >= z))(lambda i=i, z=z: pair_copy(i, z).start())

    @pl.when(to_self)
    def _():
        wbuf[KINDS * core + q] = ybuf[pl.ds(2 * (p % 4), 2)]

    @pl.when(group < GROUPS - 1)
    def _():
        remote(xbuf.at[0], xbuf.at[RING], h_send, x_recv.at[RING], m, q).wait_recv()

    halo = xbuf[RING].astype(f32).reshape(ROWS, PIECE)
    after = halo_sums(halo, run_ref, tail_ref)

    @pl.when(group == COLUMN - 1)
    def _():
        all_ref[COLUMN] = jnp.concatenate([after, jnp.zeros((7, 128), f32)], axis=0)

    x = jnp.concatenate([main, halo], axis=1)
    for j in range(SETS):
        shifted(j, x, h_ref)

    def near(i):
        block = all_ref.at[high * COLUMN + i]
        remote(block, block, s_send.at[i], s_recv.at[i], m, q).wait_recv()

    each(COLUMN, y, near)

    @pl.when(low)
    def _():
        pl.semaphore_wait(ready, 5)
        for i in range(4):
            pair_copy(i, 1).start()
        far_copy().start()


    @pl.when(high == 1)
    def _():
        block = all_ref.at[pl.ds(0, COLUMN)]
        remote(block, block, g_send, g_recv, m, q).wait_recv()

    energy = window_energy(group, all_ref, run_ref, sum_ref, tail_ref, chain_ref, outer_ref, edge_ref, part_ref)
    root_ref[...] = 1.0 / jnp.sqrt(energy + EPS)

    for cs in range(2):
        for k in range(KINDS):
            slot = KINDS * cs + k
            pl.when(comes[cs][k])(
                lambda slot=slot: remote(
                    wbuf.at[slot], wbuf.at[slot], f_send.at[0], f_recv.at[slot], m, q
                ).wait_recv()
            )
    shards = wbuf[...].astype(f32)
    shards = [shards[KINDS * cs + k, e : e + 1] for e in range(2) for cs in range(2) for k in range(KINDS)]
    sel, weight = prepare(jnp.concatenate(shards, axis=0), a_ref)
    for j in range(SETS):
        correlate(j, h_ref, a_ref, z_ref, corr_ref)

    total = stacked(root_ref[...], weight, sel, corr_ref, n_ref, z_ref)
    for i in range(RING):
        for k in range(KINDS):
            for c in range(PIECE // 128):
                at = PIECE * i + 128 * c
                part[KINDS * i + k, c : c + 1, :] = total[k : k + 1, at : at + 128]

    me = KINDS * r + q
    each(RING * KINDS, me, lambda i: part_copy(i).start())
    land[me] = part[me]
    each(RING * KINDS, me, lambda i: remote(part.at[0], land.at[i], p_send.at[i], p_recv.at[i], m, q).wait_recv())
    whole = jnp.sum(land[...], axis=0)
    for c in range(PIECE // 128):
        out_ref[:, 128 * c : 128 * c + 128] = whole[c : c + 1]

    each(COLUMN, y, lambda i: template_copy(i).wait_send())
    each(RING, r, lambda i: record_copy(i).wait_send())

    @pl.when(group > 0)
    def _():
        halo_copy().wait_send()

    for i in range(4):
        for z in range(2):
            pl.when(goes[i][z])(lambda i=i, z=z: pair_copy(i, z).wait_send())
    each(COLUMN, y, lambda i: near_copy(i).wait_send())

    @pl.when(low)
    def _():
        far_copy().wait_send()

    each(RING * KINDS, KINDS * r + q, lambda i: part_copy(i).wait_send())


def local(records, templates, shifts, valid):
    hbm = pl.BlockSpec(memory_space=pltpu.HBM)
    dma = pltpu.SemaphoreType.DMA
    return pl.pallas_call(
        kernel,
        out_shape=jax.ShapeDtypeStruct((1, PIECE), f32),
        in_specs=[hbm] * 4,
        out_specs=pl.BlockSpec(memory_space=pltpu.VMEM),
        scratch_shapes=[
            pltpu.VMEM((RING + 1, 2, ROWS // 2, PIECE), bf16),
            pltpu.VMEM((2 * KINDS, 2, 16, 256), bf16),
            pltpu.VMEM((COLUMN, 16, 256), bf16),
            pltpu.VMEM((16, 256), bf16),
            pltpu.VMEM((GROUPS, 8, 128), f32),
            pltpu.VMEM((RING * KINDS, 8, 128), f32),
            pltpu.VMEM((RING * KINDS, 8, 128), f32),
            pltpu.VMEM((1, OCT, L), bf16),
            pltpu.VMEM((2, 1, OCT), jnp.int32),
            pltpu.VMEM((SETS, 256, NH), bf16),
            pltpu.VMEM((SETS, 128, BIG), bf16),
            pltpu.VMEM((2, 128, NZ), f32),
            pltpu.VMEM((256, NZ), bf16),
            pltpu.VMEM((128, NZ), f32),
            pltpu.VMEM((1280, 128), f32),
            pltpu.VMEM((128, 128), f32),
            pltpu.VMEM((128, 128), f32),
            pltpu.VMEM((256, 128), f32),
            pltpu.VMEM((256, 128), f32),
            pltpu.VMEM((256, 128), f32),
            pltpu.VMEM((128, 128), f32),
            pltpu.VMEM((ROWS, NZ), f32),
            dma((COLUMN,)), dma((COLUMN,)),
            dma((8,)), dma((2 * KINDS,)),
            dma((RING,)), dma((RING + 1,)), dma,
            dma((COLUMN,)), dma((COLUMN,)),
            dma, dma,
            dma((RING * KINDS,)), dma((RING * KINDS,)),
            dma((4,)),
            pltpu.SemaphoreType.REGULAR,
        ],
        compiler_params=pltpu.CompilerParams(
            collective_id=0, has_side_effects=True, vmem_limit_bytes=63 * 1024 * 1024
        ),
    )(records.reshape(GROUPS, 4, 16, PIECE), templates, shifts, valid)


def solution(mesh):
    in_specs = (P(None, "tm"), P("tmpl", "tm", None), P("tmpl", "tm"), P("tmpl", "tm"))
    return jax.shard_map(local, mesh=mesh, in_specs=in_specs, out_specs=P("tmpl", "tm"), check_vma=False)
```

```python
import functools

import jax
import jax.numpy as jnp
from jax import lax
from jax.experimental import pallas as pl
from jax.experimental.pallas import tpu as pltpu
from jax.sharding import PartitionSpec as P

L = 300
MAXS = 20
EPS = 1e-05
KINDS = 4
RING = 8
GROUPS = 16
COLUMN = 8
PIECE = 384
ROWS = 32
OCT = 8
SETS = ROWS // OCT
STEP = 32
SPAN = RING * PIECE
WIDE = SPAN + PIECE
NH = 3584
NZ = 3328
BIG = 3 * 256
QUARTER = SPAN // 4
LEVELS = 22
BLOCKS = (WIDE // 16)
CHAIN = 208

f32 = jnp.float32
bf16 = jnp.bfloat16


def prepare(taps, a_ref):
    pairs = SETS * KINDS * OCT
    third = jnp.where(lax.broadcasted_iota(jnp.int32, (pairs, 128), 1) < L - 256, taps[:, 256:], 0.0)
    thirds = [taps[:, :128], taps[:, 128:256], third]

    parts = [part.astype(bf16) for part in thirds]
    lane = lax.broadcasted_iota(jnp.int32, (128, 256), 1)
    line = lax.broadcasted_iota(jnp.int32, (128, 256), 0)
    same = (lane % OCT) == (line % OCT)
    for u_lo in range(4):
        spread = jnp.where(line == STEP * u_lo + lane // OCT, 1.0, 0.0).astype(bf16)
        for u_hi in range(3):
            wide = jnp.dot(parts[u_hi], spread, preferred_element_type=f32)
            block = jnp.where(same, wide, 0.0).astype(bf16)
            for j in range(SETS):
                a_ref[j, 32 * u_lo : 32 * u_lo + 32, 256 * u_hi : 256 * u_hi + 256] = block[32 * j : 32 * j + 32]

    shift = taps[:, L : L + 1]
    valid = taps[:, L + 1 : L + 2]
    column = lax.broadcasted_iota(jnp.int32, (pairs, 128), 1)
    squares = thirds[0] ** 2 + thirds[1] ** 2 + thirds[2] ** 2
    power = jnp.sum(squares, axis=1, keepdims=True) / L
    weight = valid / (L * jnp.sqrt(power + EPS))

    kind = (lax.broadcasted_iota(jnp.int32, (pairs, 128), 0) // OCT) % KINDS
    picked = (shift == (column // KINDS).astype(f32)) & (kind == column % KINDS)
    sel = jnp.transpose(jnp.where(picked, 1.0, 0.0)).astype(bf16)
    return jnp.concatenate([sel, sel], axis=1)[: 4 * LEVELS], weight


def shifted(j, x, h_ref):
    x8 = jnp.concatenate([x[OCT * j : OCT * j + OCT], jnp.zeros((OCT, NH - WIDE), f32)], axis=1)
    for i in range(STEP // 2):
        first = x8 if i == 0 else pltpu.roll(x8, NH - 2 * i, 1)
        second = pltpu.roll(x8, NH - 2 * i - 1, 1)
        h_ref[j, 16 * i : 16 * i + 16, :] = jnp.concatenate([first, second], axis=0).astype(bf16)


def correlate(j, h_ref, a_ref, z_ref, corr_ref):
    slot = j % 2
    for n in range(NZ // 256):
        acc = None
        for u_hi in range(3):
            part = jnp.dot(
                a_ref[j, :, 256 * u_hi : 256 * u_hi + 256],
                h_ref[j, :, 256 * n + 128 * u_hi : 256 * n + 128 * u_hi + 256],
                preferred_element_type=f32,
            )
            acc = part if acc is None else acc + part
        z_ref[slot, :, 256 * n : 256 * n + 256] = acc
    for k in range(KINDS):
        corr = z_ref[slot, 8 * k : 8 * k + 8, :]
        for u_lo in range(1, 4):
            corr = corr + pltpu.roll(z_ref[slot, 32 * u_lo + 8 * k : 32 * u_lo + 8 * k + 8, :], NZ - STEP * u_lo, 1)
        corr_ref[32 * j + 8 * k : 32 * j + 8 * k + 8, :] = corr


def running16(run_ref, start, rows, sum_ref):
    acc = run_ref[pl.ds(start, rows, stride=16), :]
    for d in range(1, 16):
        acc = acc + run_ref[pl.ds(start + d, rows, stride=16), :]
        run_ref[pl.ds(start + d, rows, stride=16), :] = acc
    sum_ref[:rows, :] = acc
    sum_ref[rows:, :] = jnp.zeros((128 - rows, 128), f32)
    outer = sum_ref[pl.ds(0, 8, stride=16), :]
    for c in range(1, 16):
        outer = outer + sum_ref[pl.ds(c, 8, stride=16), :]
        sum_ref[pl.ds(c, 8, stride=16), :] = outer
    return acc, outer


def block_sums(x, run_ref, sum_ref):
    squares = x * x
    stacked = jnp.concatenate([squares[:, QUARTER * s : QUARTER * s + QUARTER] for s in range(4)], axis=0)
    for i in range(QUARTER // 128):
        run_ref[128 * i : 128 * i + 128, :] = jnp.transpose(stacked[:, 128 * i : 128 * i + 128])
    acc, outer = running16(run_ref, 0, QUARTER // 16, sum_ref)
    final = acc[QUARTER // 16 - 1 : QUARTER // 16]
    before = sum_ref[QUARTER // 16 - 2 : QUARTER // 16 - 1, :]
    return jnp.concatenate([outer[:3], final, before, jnp.zeros((3, 128), f32)], axis=0)


def halo_sums(x, run_ref, tail_ref):
    halo = jnp.concatenate([x * x, jnp.zeros((128 - ROWS, PIECE), f32)], axis=0)
    for i in range(PIECE // 128):
        run_ref[QUARTER + 128 * i : QUARTER + 128 * i + 128, :] = jnp.transpose(halo[:, 128 * i : 128 * i + 128])
    _, outer = running16(run_ref, QUARTER, PIECE // 16, tail_ref)
    return outer[:1]


def window_energy(group, all_ref, run_ref, sum_ref, tail_ref, chain_ref, outer_ref, edge_ref, part_ref):
    for g in range(GROUPS):
        totals = all_ref[g]
        for s in range(4):
            moved = totals if s == 0 else pltpu.roll(totals, 128 - ROWS * s, 1)
            chain_ref[12 * g + 3 * s : 12 * g + 3 * s + 3, :] = moved[:3]
    chain_ref[12 * GROUPS :, :] = jnp.zeros((256 - 12 * GROUPS, 128), f32)
    plain = chain_ref[:CHAIN, :]
    acc = chain_ref[pl.ds(0, 16, stride=16), :]
    for b in range(1, 16):
        acc = acc + chain_ref[pl.ds(b, 16, stride=16), :]
        chain_ref[pl.ds(b, 16, stride=16), :] = acc
    outer_ref[:8, :] = jnp.zeros((8, 128), f32)
    top = jnp.zeros((1, 128), f32)
    for a in range(CHAIN // 16):
        outer_ref[16 * a + 9 : 16 * a + 25, :] = chain_ref[16 * a : 16 * a + 16, :] + top
        top = top + acc[a : a + 1]
    outer_ref[8:9, :] = jnp.zeros((1, 128), f32)
    edge_ref[:8, :] = jnp.zeros((8, 128), f32)
    edge_ref[9 : 9 + CHAIN, :] = plain + outer_ref[8 : 8 + CHAIN, :]
    edge_ref[8:9, :] = jnp.zeros((1, 128), f32)
    mine = outer_ref[7:23, :]
    edge = edge_ref[7:23, :]
    for g in range(1, GROUPS):
        here = group == g
        mine = jnp.where(here, outer_ref[12 * g + 7 : 12 * g + 23, :], mine)
        edge = jnp.where(here, edge_ref[12 * g + 7 : 12 * g + 23, :], edge)
    lane = lax.broadcasted_iota(jnp.int32, (1, 128), 1) // ROWS

    def spread(rows, b):
        out = rows[1 + b : 2 + b]
        for s in range(1, 4):
            out = jnp.where(lane == s, pltpu.roll(rows[1 + 3 * s + b : 2 + 3 * s + b], ROWS * s, 1), out)
        return out

    befores = [spread(mine, b) for b in range(3)] + [mine[13:14], mine[14:15]]
    edges = [spread(edge, b) for b in range(3)] + [edge[13:14], edge[14:15]]
    for b in range(5):
        sums = sum_ref[16 * b : 16 * b + 16, :] if b < 3 else tail_ref[16 * b - 48 : 16 * b - 32, :]
        part_ref[16 * b + 1 : 16 * b + 17, :] = sums + befores[b]
        part_ref[16 * b : 16 * b + 1, :] = edges[b]
    quarter = QUARTER
    rows = (quarter + PIECE) // 16
    base = part_ref[:rows, :]
    for d in range(16):
        run_ref[pl.ds(d, rows, stride=16), :] = run_ref[pl.ds(d, rows, stride=16), :] + base
    ahead = pltpu.roll(all_ref[jnp.maximum(group - 1, 0)], ROWS, 1)
    last = jnp.where(group > 0, ahead[3:4] + (ahead[4:5] + mine[0:1]), 0.0)
    stretch = quarter + PIECE
    run_ref[stretch : stretch + 128, :] = jnp.concatenate([jnp.zeros((127, 128), f32), last], axis=0)
    main = jnp.concatenate(
        [jnp.transpose(run_ref[128 * i : 128 * i + 128, :]) for i in range(quarter // 128)], axis=1
    )
    tail = [jnp.transpose(run_ref[quarter + 128 * i : quarter + 128 * i + 128, :])[:ROWS] for i in range(4)]
    running = jnp.concatenate([main[ROWS * s : ROWS * s + ROWS] for s in range(4)] + tail, axis=1)
    energy = pltpu.roll(running, NH - (L - 1), 1) - pltpu.roll(running, 1, 1)
    return jnp.maximum(energy, 0.0)[:, :NZ] / L


def stacked(inverse, weight, sel, corr_ref, n_ref, z_ref):
    pairs = SETS * KINDS * OCT
    for j in range(SETS):
        for k in range(KINDS):
            row = 32 * j + 8 * k
            corr_ref[row : row + 8, :] = corr_ref[row : row + 8, :] * inverse[OCT * j : OCT * j + OCT] * weight[row : row + 8]
        normed = corr_ref[32 * j : 32 * j + 32, :]
        head = normed.astype(bf16)
        n_ref[32 * j : 32 * j + 32, :] = head
        n_ref[pairs + 32 * j : pairs + 32 * j + 32, :] = (normed - head.astype(f32)).astype(bf16)
    for n in range(NZ // 256):
        z_ref[0, : 4 * LEVELS, 256 * n : 256 * n + 256] = jnp.dot(
            sel, n_ref[:, 256 * n : 256 * n + 256], preferred_element_type=f32
        )
    total = z_ref[0, :8, :]
    for i in range(1, LEVELS // 2):
        total = total + pltpu.roll(z_ref[0, 8 * i : 8 * i + 8, :], NZ - 2 * i, 1)
    return total + pltpu.roll(pltpu.roll(total, NZ - 1, 1), 4, 0)


def kernel(
    rec_ref, tmpl_ref, shift_ref, valid_ref, out_ref,
    xbuf, wbuf, ybuf, pair, msg, all_ref, part, land, tbuf, ibuf,
    h_ref, a_ref, z_ref, n_ref, corr_ref, run_ref, sum_ref, tail_ref, chain_ref, outer_ref, edge_ref, part_ref, root_ref,
    w_send, w_recv, f_send, f_recv, x_send, x_recv, h_send, s_send, s_recv, g_send, g_recv,
    p_send, p_recv, own, ready,
):
    m, q = lax.axis_index("tm"), lax.axis_index("tmpl")
    group, r = m // RING, m % RING
    high, y = group // COLUMN, group % COLUMN
    x_at, core = r // 2, r % 2
    p = 2 * q + core
    to_self = p // 4 == high
    barrier = pltpu.get_barrier_semaphore()

    def signal(tm, tmpl):
        pl.semaphore_signal(barrier, inc=1, device_id=(tm, tmpl), device_id_type=pl.DeviceIdType.MESH)

    def remote(src, dst, send, recv, tm, tmpl):
        return pltpu.make_async_remote_copy(
            src_ref=src, dst_ref=dst, send_sem=send, recv_sem=recv,
            device_id=(tm, tmpl), device_id_type=pl.DeviceIdType.MESH,
        )

    def each(count, skip, step):
        for i in range(count):
            pl.when(i != skip)(functools.partial(step, i))

    def at_y(i):
        return (high * COLUMN + i) * RING + r

    local = [
        pltpu.make_async_copy(tmpl_ref, tbuf, own.at[0]),
        pltpu.make_async_copy(shift_ref, ibuf.at[0], own.at[1]),
        pltpu.make_async_copy(valid_ref, ibuf.at[1], own.at[2]),
        pltpu.make_async_copy(rec_ref.at[pl.ds(2 * p, 2), x_at], xbuf.at[r], own.at[3]),
    ]
    for copy in local:
        copy.start()

    low = high == 0
    other = (1 - high) * COLUMN * RING + y * RING + r

    def pair_target(i, z):
        return (z * COLUMN + y) * RING + 2 * x_at + i % 2, 2 * high + i // 2

    @pl.when(low)
    def _():
        signal(other, q)
        for i in range(4):
            signal(*pair_target(i, 1))

    each(COLUMN, y, lambda i: signal(at_y(i), q))
    comes = [
        [jnp.logical_not(to_self & (core == cs) & (q == k)) for k in range(KINDS)] for cs in range(2)
    ]
    for cs in range(2):
        for k in range(KINDS):
            source = ((p // 4) * COLUMN + y) * RING + 2 * x_at + cs
            pl.when(comes[cs][k] & (low | to_self))(functools.partial(signal, source, k))
    each(RING * KINDS, KINDS * r + q, lambda i: signal(group * RING + i // KINDS, i % KINDS))

    @pl.when(group < GROUPS - 1)
    def _():
        signal(m + RING, q)

    for copy in local[:3]:
        copy.wait()

    waves = tbuf[0].astype(f32)
    eye = lax.broadcasted_iota(jnp.int32, (OCT, OCT), 0) == lax.broadcasted_iota(jnp.int32, (OCT, OCT), 1)
    moves = jnp.sum(jnp.where(eye, ibuf[0].astype(f32), 0.0), axis=1, keepdims=True)
    masks = jnp.sum(jnp.where(eye, ibuf[1].astype(f32), 0.0), axis=1, keepdims=True)
    lane = lax.broadcasted_iota(jnp.int32, (OCT, 128), 1)
    tail = jnp.concatenate([waves[:, 256:], jnp.zeros((OCT, 128 - (L - 256)), f32)], axis=1)
    tail = jnp.where(lane == L - 256, moves, jnp.where(lane == L - 255, masks, tail))
    tail = jnp.concatenate([tail, jnp.zeros((OCT, 128), f32)], axis=1)
    msg[...] = jnp.concatenate([waves[:, :256], tail], axis=0).astype(bf16)

    @pl.when(group == GROUPS - 1)
    def _():
        xbuf[RING] = jnp.zeros((2, ROWS // 2, PIECE), bf16)

    count = (
        (COLUMN - 1) + 4 - to_self.astype(jnp.int32)
        + (RING * KINDS - 1) + (group > 0).astype(jnp.int32)
        + high * (5 + 8 * (1 - to_self.astype(jnp.int32)))
    )

    @pl.when(low)
    def _():
        all_ref[COLUMN:] = jnp.zeros((COLUMN, 8, 128), f32)

    pl.semaphore_wait(barrier, count)

    def answer(tm, tmpl):
        pl.semaphore_signal(ready, inc=1, device_id=(tm, tmpl), device_id_type=pl.DeviceIdType.MESH)

    @pl.when(high == 1)
    def _():
        answer(other, q)

    @pl.when((high == 1) & jnp.logical_not(to_self))
    def _():
        for cs in range(2):
            for k in range(KINDS):
                answer(y * RING + 2 * x_at + cs, k)

    def record(i):
        return rec_ref.at[pl.ds(2 * (2 * q + i % 2), 2), i // 2]

    def template_copy(i):
        return remote(msg, ybuf.at[y], w_send.at[i], w_recv.at[y], at_y(i), q)

    def pair_copy(i, z):
        return remote(
            pair.at[i], wbuf.at[KINDS * core + q], f_send.at[2 * i + z], f_recv.at[KINDS * core + q],
            *pair_target(i, z),
        )

    def record_copy(i):
        return remote(record(i), xbuf.at[r], x_send.at[i], x_recv.at[r], group * RING + i, q)

    def halo_copy():
        return remote(xbuf.at[0], xbuf.at[RING], h_send, x_recv.at[RING], m - RING, q)

    def near_copy(i):
        return remote(all_ref.at[group], all_ref.at[group], s_send.at[i], s_recv.at[y], at_y(i), q)

    def far_copy():
        block = all_ref.at[pl.ds(COLUMN * high, COLUMN)]
        return remote(block, block, g_send, g_recv, other, q)

    def part_copy(i):
        me = KINDS * r + q
        return remote(
            part.at[i, pl.ds(0, 3)], land.at[me, pl.ds(0, 3)], p_send.at[i], p_recv.at[me], group * RING + i // KINDS, i % KINDS
        )

    goes = [[jnp.logical_not(to_self & (p % 4 == i) & (high == z)) for z in range(2)] for i in range(4)]

    each(COLUMN, y, lambda i: template_copy(i).start())
    each(RING, r, lambda i: record_copy(i).start())
    ybuf[y] = msg[...]
    local[3].wait()
    each(RING, r, lambda i: remote(xbuf.at[i], xbuf.at[i], x_send.at[i], x_recv.at[i], m, q).wait_recv())

    @pl.when(group > 0)
    def _():
        halo_copy().start()

    main = jnp.concatenate([xbuf[i].astype(f32).reshape(ROWS, PIECE) for i in range(RING)], axis=1)
    all_ref[group] = block_sums(main, run_ref, sum_ref)
    each(COLUMN, y, lambda i: near_copy(i).start())

    each(COLUMN, y, lambda i: remote(msg, ybuf.at[i], w_send.at[i], w_recv.at[i], m, q).wait_recv())
    for i in range(4):
        both = [ybuf[2 * i + e].astype(f32) for e in range(2)]
        both = [jnp.concatenate([one[:OCT], one[OCT:, :128]], axis=1) for one in both]
        pair[i] = jnp.concatenate(both, axis=0).astype(bf16)
    for z in range(2):
        for i in range(4):
            pl.when(goes[i][z] & (high >= z))(lambda i=i, z=z: pair_copy(i, z).start())

    @pl.when(to_self)
    def _():
        wbuf[KINDS * core + q] = pair[p % 4]

    @pl.when(group < GROUPS - 1)
    def _():
        remote(xbuf.at[0], xbuf.at[RING], h_send, x_recv.at[RING], m, q).wait_recv()

    halo = xbuf[RING].astype(f32).reshape(ROWS, PIECE)
    after = halo_sums(halo, run_ref, tail_ref)

    @pl.when(group == COLUMN - 1)
    def _():
        all_ref[COLUMN] = jnp.concatenate([after, jnp.zeros((7, 128), f32)], axis=0)

    x = jnp.concatenate([main, halo], axis=1)
    for j in range(SETS):
        shifted(j, x, h_ref)

    def near(i):
        block = all_ref.at[high * COLUMN + i]
        remote(block, block, s_send.at[i], s_recv.at[i], m, q).wait_recv()

    each(COLUMN, y, near)

    @pl.when(low)
    def _():
        pl.semaphore_wait(ready, 5)
        for i in range(4):
            pair_copy(i, 1).start()
        far_copy().start()


    @pl.when(high == 1)
    def _():
        block = all_ref.at[pl.ds(0, COLUMN)]
        remote(block, block, g_send, g_recv, m, q).wait_recv()

    energy = window_energy(group, all_ref, run_ref, sum_ref, tail_ref, chain_ref, outer_ref, edge_ref, part_ref)
    root_ref[...] = 1.0 / jnp.sqrt(energy + EPS)

    for cs in range(2):
        for k in range(KINDS):
            slot = KINDS * cs + k
            pl.when(comes[cs][k])(
                lambda slot=slot: remote(
                    wbuf.at[slot], wbuf.at[slot], f_send.at[0], f_recv.at[slot], m, q
                ).wait_recv()
            )
    shards = wbuf[...].astype(f32)
    shards = [
        shards[KINDS * cs + k, OCT * e : OCT * e + OCT] for e in range(2) for cs in range(2) for k in range(KINDS)
    ]
    sel, weight = prepare(jnp.concatenate(shards, axis=0), a_ref)
    for j in range(SETS):
        correlate(j, h_ref, a_ref, z_ref, corr_ref)

    total = stacked(root_ref[...], weight, sel, corr_ref, n_ref, z_ref)
    for i in range(RING):
        for k in range(KINDS):
            for c in range(PIECE // 128):
                at = PIECE * i + 128 * c
                part[KINDS * i + k, c : c + 1, :] = total[k : k + 1, at : at + 128]

    me = KINDS * r + q
    each(RING * KINDS, me, lambda i: part_copy(i).start())
    land[me, :3] = part[me, :3]
    each(RING * KINDS, me, lambda i: remote(part.at[0, pl.ds(0, 3)], land.at[i, pl.ds(0, 3)], p_send.at[i], p_recv.at[i], m, q).wait_recv())
    whole = jnp.sum(land[:, :3], axis=0)
    for c in range(PIECE // 128):
        out_ref[:, 128 * c : 128 * c + 128] = whole[c : c + 1]

    each(COLUMN, y, lambda i: template_copy(i).wait_send())
    each(RING, r, lambda i: record_copy(i).wait_send())

    @pl.when(group > 0)
    def _():
        halo_copy().wait_send()

    for i in range(4):
        for z in range(2):
            pl.when(goes[i][z])(lambda i=i, z=z: pair_copy(i, z).wait_send())
    each(COLUMN, y, lambda i: near_copy(i).wait_send())

    @pl.when(low)
    def _():
        far_copy().wait_send()

    each(RING * KINDS, KINDS * r + q, lambda i: part_copy(i).wait_send())


def local(records, templates, shifts, valid):
    hbm = pl.BlockSpec(memory_space=pltpu.HBM)
    dma = pltpu.SemaphoreType.DMA
    return pl.pallas_call(
        kernel,
        out_shape=jax.ShapeDtypeStruct((1, PIECE), f32),
        in_specs=[hbm] * 4,
        out_specs=pl.BlockSpec(memory_space=pltpu.VMEM),
        scratch_shapes=[
            pltpu.VMEM((RING + 1, 2, ROWS // 2, PIECE), bf16),
            pltpu.VMEM((2 * KINDS, 16, 384), bf16),
            pltpu.VMEM((COLUMN, 16, 256), bf16),
            pltpu.VMEM((4, 16, 384), bf16),
            pltpu.VMEM((16, 256), bf16),
            pltpu.VMEM((GROUPS, 8, 128), f32),
            pltpu.VMEM((RING * KINDS, 8, 128), f32),
            pltpu.VMEM((RING * KINDS, 8, 128), f32),
            pltpu.VMEM((1, OCT, L), bf16),
            pltpu.VMEM((2, 1, OCT), jnp.int32),
            pltpu.VMEM((SETS, 256, NH), bf16),
            pltpu.VMEM((SETS, 128, BIG), bf16),
            pltpu.VMEM((2, 128, NZ), f32),
            pltpu.VMEM((256, NZ), bf16),
            pltpu.VMEM((128, NZ), f32),
            pltpu.VMEM((1280, 128), f32),
            pltpu.VMEM((128, 128), f32),
            pltpu.VMEM((128, 128), f32),
            pltpu.VMEM((256, 128), f32),
            pltpu.VMEM((256, 128), f32),
            pltpu.VMEM((256, 128), f32),
            pltpu.VMEM((128, 128), f32),
            pltpu.VMEM((ROWS, NZ), f32),
            dma((COLUMN,)), dma((COLUMN,)),
            dma((8,)), dma((2 * KINDS,)),
            dma((RING,)), dma((RING + 1,)), dma,
            dma((COLUMN,)), dma((COLUMN,)),
            dma, dma,
            dma((RING * KINDS,)), dma((RING * KINDS,)),
            dma((4,)),
            pltpu.SemaphoreType.REGULAR,
        ],
        compiler_params=pltpu.CompilerParams(
            collective_id=0, has_side_effects=True, vmem_limit_bytes=63 * 1024 * 1024
        ),
    )(records.reshape(GROUPS, 4, 16, PIECE), templates, shifts, valid)


def solution(mesh):
    in_specs = (P(None, "tm"), P("tmpl", "tm", None), P("tmpl", "tm"), P("tmpl", "tm"))
    return jax.shard_map(local, mesh=mesh, in_specs=in_specs, out_specs=P("tmpl", "tm"), check_vma=False)
```

```python
import functools

import jax
import jax.numpy as jnp
from jax import lax
from jax.experimental import pallas as pl
from jax.experimental.pallas import tpu as pltpu
from jax.sharding import PartitionSpec as P

L = 300
MAXS = 20
EPS = 1e-05
KINDS = 4
RING = 8
GROUPS = 16
COLUMN = 8
PIECE = 384
ROWS = 32
OCT = 8
SETS = ROWS // OCT
STEP = 32
SPAN = RING * PIECE
WIDE = SPAN + PIECE
NH = 3584
NZ = 3328
BIG = 3 * 256
QUARTER = SPAN // 4
EARLY = SPAN - 128
LEVELS = 22
BLOCKS = (WIDE // 16)
CHAIN = 208

f32 = jnp.float32
bf16 = jnp.bfloat16


def prepare(taps, a_ref):
    pairs = SETS * KINDS * OCT
    third = jnp.where(lax.broadcasted_iota(jnp.int32, (pairs, 128), 1) < L - 256, taps[:, 256:], 0.0)
    thirds = [taps[:, :128], taps[:, 128:256], third]

    parts = [part.astype(bf16) for part in thirds]
    lane = lax.broadcasted_iota(jnp.int32, (128, 256), 1)
    line = lax.broadcasted_iota(jnp.int32, (128, 256), 0)
    same = (lane % OCT) == (line % OCT)
    for u_lo in range(4):
        spread = jnp.where(line == STEP * u_lo + lane // OCT, 1.0, 0.0).astype(bf16)
        for u_hi in range(3):
            wide = jnp.dot(parts[u_hi], spread, preferred_element_type=f32)
            block = jnp.where(same, wide, 0.0).astype(bf16)
            for j in range(SETS):
                a_ref[j, 32 * u_lo : 32 * u_lo + 32, 256 * u_hi : 256 * u_hi + 256] = block[32 * j : 32 * j + 32]

    shift = taps[:, L : L + 1]
    valid = taps[:, L + 1 : L + 2]
    column = lax.broadcasted_iota(jnp.int32, (pairs, 128), 1)
    squares = thirds[0] ** 2 + thirds[1] ** 2 + thirds[2] ** 2
    power = jnp.sum(squares, axis=1, keepdims=True) / L
    weight = valid / (L * jnp.sqrt(power + EPS))

    kind = (lax.broadcasted_iota(jnp.int32, (pairs, 128), 0) // OCT) % KINDS
    picked = (shift == (column // KINDS).astype(f32)) & (kind == column % KINDS)
    sel = jnp.transpose(jnp.where(picked, 1.0, 0.0)).astype(bf16)
    return jnp.concatenate([sel, sel], axis=1)[: 4 * LEVELS], weight


def shifted(j, x, h_ref, start, keep):
    x8 = x[OCT * j : OCT * j + OCT]
    wide = x8.shape[1]
    for i in range(STEP // 2):
        first = x8 if i == 0 else pltpu.roll(x8, wide - 2 * i, 1)
        second = pltpu.roll(x8, wide - 2 * i - 1, 1)
        both = jnp.concatenate([first[:, :keep], second[:, :keep]], axis=0)
        h_ref[j, 16 * i : 16 * i + 16, start : start + keep] = both.astype(bf16)


def correlate(j, h_ref, a_ref, z_ref, corr_ref):
    slot = j % 2
    for n in range(NZ // 256):
        acc = None
        for u_hi in range(3):
            part = jnp.dot(
                a_ref[j, :, 256 * u_hi : 256 * u_hi + 256],
                h_ref[j, :, 256 * n + 128 * u_hi : 256 * n + 128 * u_hi + 256],
                preferred_element_type=f32,
            )
            acc = part if acc is None else acc + part
        z_ref[slot, :, 256 * n : 256 * n + 256] = acc
    for k in range(KINDS):
        corr = z_ref[slot, 8 * k : 8 * k + 8, :]
        for u_lo in range(1, 4):
            corr = corr + pltpu.roll(z_ref[slot, 32 * u_lo + 8 * k : 32 * u_lo + 8 * k + 8, :], NZ - STEP * u_lo, 1)
        corr_ref[32 * j + 8 * k : 32 * j + 8 * k + 8, :] = corr


def running16(run_ref, start, rows, sum_ref):
    acc = run_ref[pl.ds(start, rows, stride=16), :]
    for d in range(1, 16):
        acc = acc + run_ref[pl.ds(start + d, rows, stride=16), :]
        run_ref[pl.ds(start + d, rows, stride=16), :] = acc
    sum_ref[:rows, :] = acc
    sum_ref[rows:, :] = jnp.zeros((128 - rows, 128), f32)
    outer = sum_ref[pl.ds(0, 8, stride=16), :]
    for c in range(1, 16):
        outer = outer + sum_ref[pl.ds(c, 8, stride=16), :]
        sum_ref[pl.ds(c, 8, stride=16), :] = outer
    return acc, outer


def block_sums(x, run_ref, sum_ref):
    squares = x * x
    stacked = jnp.concatenate([squares[:, QUARTER * s : QUARTER * s + QUARTER] for s in range(4)], axis=0)
    for i in range(QUARTER // 128):
        run_ref[128 * i : 128 * i + 128, :] = jnp.transpose(stacked[:, 128 * i : 128 * i + 128])
    acc, outer = running16(run_ref, 0, QUARTER // 16, sum_ref)
    final = acc[QUARTER // 16 - 1 : QUARTER // 16]
    before = sum_ref[QUARTER // 16 - 2 : QUARTER // 16 - 1, :]
    return jnp.concatenate([outer[:3], final, before, jnp.zeros((3, 128), f32)], axis=0)


def halo_sums(x, run_ref, tail_ref):
    halo = jnp.concatenate([x * x, jnp.zeros((128 - ROWS, PIECE), f32)], axis=0)
    for i in range(PIECE // 128):
        run_ref[QUARTER + 128 * i : QUARTER + 128 * i + 128, :] = jnp.transpose(halo[:, 128 * i : 128 * i + 128])
    _, outer = running16(run_ref, QUARTER, PIECE // 16, tail_ref)
    return outer[:1]


def window_energy(group, all_ref, run_ref, sum_ref, tail_ref, chain_ref, outer_ref, edge_ref, part_ref):
    for g in range(GROUPS):
        totals = all_ref[g]
        for s in range(4):
            moved = totals if s == 0 else pltpu.roll(totals, 128 - ROWS * s, 1)
            chain_ref[12 * g + 3 * s : 12 * g + 3 * s + 3, :] = moved[:3]
    chain_ref[12 * GROUPS :, :] = jnp.zeros((256 - 12 * GROUPS, 128), f32)
    plain = chain_ref[:CHAIN, :]
    acc = chain_ref[pl.ds(0, 16, stride=16), :]
    for b in range(1, 16):
        acc = acc + chain_ref[pl.ds(b, 16, stride=16), :]
        chain_ref[pl.ds(b, 16, stride=16), :] = acc
    outer_ref[:8, :] = jnp.zeros((8, 128), f32)
    top = jnp.zeros((1, 128), f32)
    for a in range(CHAIN // 16):
        outer_ref[16 * a + 9 : 16 * a + 25, :] = chain_ref[16 * a : 16 * a + 16, :] + top
        top = top + acc[a : a + 1]
    outer_ref[8:9, :] = jnp.zeros((1, 128), f32)
    edge_ref[:8, :] = jnp.zeros((8, 128), f32)
    edge_ref[9 : 9 + CHAIN, :] = plain + outer_ref[8 : 8 + CHAIN, :]
    edge_ref[8:9, :] = jnp.zeros((1, 128), f32)
    mine = outer_ref[7:23, :]
    edge = edge_ref[7:23, :]
    for g in range(1, GROUPS):
        here = group == g
        mine = jnp.where(here, outer_ref[12 * g + 7 : 12 * g + 23, :], mine)
        edge = jnp.where(here, edge_ref[12 * g + 7 : 12 * g + 23, :], edge)
    lane = lax.broadcasted_iota(jnp.int32, (1, 128), 1) // ROWS

    def spread(rows, b):
        out = rows[1 + b : 2 + b]
        for s in range(1, 4):
            out = jnp.where(lane == s, pltpu.roll(rows[1 + 3 * s + b : 2 + 3 * s + b], ROWS * s, 1), out)
        return out

    befores = [spread(mine, b) for b in range(3)] + [mine[13:14], mine[14:15]]
    edges = [spread(edge, b) for b in range(3)] + [edge[13:14], edge[14:15]]
    for b in range(5):
        sums = sum_ref[16 * b : 16 * b + 16, :] if b < 3 else tail_ref[16 * b - 48 : 16 * b - 32, :]
        part_ref[16 * b + 1 : 16 * b + 17, :] = sums + befores[b]
        part_ref[16 * b : 16 * b + 1, :] = edges[b]
    quarter = QUARTER
    rows = (quarter + PIECE) // 16
    base = part_ref[:rows, :]
    for d in range(16):
        run_ref[pl.ds(d, rows, stride=16), :] = run_ref[pl.ds(d, rows, stride=16), :] + base
    ahead = pltpu.roll(all_ref[jnp.maximum(group - 1, 0)], ROWS, 1)
    last = jnp.where(group > 0, ahead[3:4] + (ahead[4:5] + mine[0:1]), 0.0)
    stretch = quarter + PIECE
    run_ref[stretch : stretch + 128, :] = jnp.concatenate([jnp.zeros((127, 128), f32), last], axis=0)
    main = jnp.concatenate(
        [jnp.transpose(run_ref[128 * i : 128 * i + 128, :]) for i in range(quarter // 128)], axis=1
    )
    tail = [jnp.transpose(run_ref[quarter + 128 * i : quarter + 128 * i + 128, :])[:ROWS] for i in range(4)]
    running = jnp.concatenate([main[ROWS * s : ROWS * s + ROWS] for s in range(4)] + tail, axis=1)
    energy = pltpu.roll(running, NH - (L - 1), 1) - pltpu.roll(running, 1, 1)
    return jnp.maximum(energy, 0.0)[:, :NZ] / L


def stacked(inverse, weight, sel, corr_ref, n_ref, z_ref):
    pairs = SETS * KINDS * OCT
    for j in range(SETS):
        for k in range(KINDS):
            row = 32 * j + 8 * k
            corr_ref[row : row + 8, :] = corr_ref[row : row + 8, :] * inverse[OCT * j : OCT * j + OCT] * weight[row : row + 8]
        normed = corr_ref[32 * j : 32 * j + 32, :]
        head = normed.astype(bf16)
        n_ref[32 * j : 32 * j + 32, :] = head
        n_ref[pairs + 32 * j : pairs + 32 * j + 32, :] = (normed - head.astype(f32)).astype(bf16)
    for n in range(NZ // 256):
        z_ref[0, : 4 * LEVELS, 256 * n : 256 * n + 256] = jnp.dot(
            sel, n_ref[:, 256 * n : 256 * n + 256], preferred_element_type=f32
        )
    total = z_ref[0, :8, :]
    for i in range(1, LEVELS // 2):
        total = total + pltpu.roll(z_ref[0, 8 * i : 8 * i + 8, :], NZ - 2 * i, 1)
    return total + pltpu.roll(pltpu.roll(total, NZ - 1, 1), 4, 0)


def kernel(
    rec_ref, tmpl_ref, shift_ref, valid_ref, out_ref,
    xbuf, wbuf, ybuf, pair, msg, all_ref, part, land, tbuf, ibuf,
    h_ref, a_ref, z_ref, n_ref, corr_ref, run_ref, sum_ref, tail_ref, chain_ref, outer_ref, edge_ref, part_ref, root_ref,
    w_send, w_recv, f_send, f_recv, x_send, x_recv, h_send, e_send, s_send, s_recv, g_send, g_recv,
    p_send, p_recv, own, ready,
):
    m, q = lax.axis_index("tm"), lax.axis_index("tmpl")
    group, r = m // RING, m % RING
    high, y = group // COLUMN, group % COLUMN
    x_at, core = r // 2, r % 2
    p = 2 * q + core
    to_self = p // 4 == high
    barrier = pltpu.get_barrier_semaphore()

    def signal(tm, tmpl):
        pl.semaphore_signal(barrier, inc=1, device_id=(tm, tmpl), device_id_type=pl.DeviceIdType.MESH)

    def remote(src, dst, send, recv, tm, tmpl):
        return pltpu.make_async_remote_copy(
            src_ref=src, dst_ref=dst, send_sem=send, recv_sem=recv,
            device_id=(tm, tmpl), device_id_type=pl.DeviceIdType.MESH,
        )

    def each(count, skip, step):
        for i in range(count):
            pl.when(i != skip)(functools.partial(step, i))

    def at_y(i):
        return (high * COLUMN + i) * RING + r

    local = [
        pltpu.make_async_copy(tmpl_ref, tbuf, own.at[0]),
        pltpu.make_async_copy(shift_ref, ibuf.at[0], own.at[1]),
        pltpu.make_async_copy(valid_ref, ibuf.at[1], own.at[2]),
        pltpu.make_async_copy(rec_ref.at[pl.ds(2 * p, 2), x_at], xbuf.at[r], own.at[3]),
    ]
    for copy in local:
        copy.start()

    low = high == 0
    passes = (group > 0) & (group != COLUMN)
    head = m == COLUMN * RING
    other = (1 - high) * COLUMN * RING + y * RING + r

    def pair_target(i, z):
        return (z * COLUMN + y) * RING + 2 * x_at + i % 2, 2 * high + i // 2

    @pl.when(low)
    def _():
        signal(other, q)
        for i in range(4):
            signal(*pair_target(i, 1))

    each(COLUMN, y, lambda i: signal(at_y(i), q))
    comes = [
        [jnp.logical_not(to_self & (core == cs) & (q == k)) for k in range(KINDS)] for cs in range(2)
    ]
    for cs in range(2):
        for k in range(KINDS):
            source = ((p // 4) * COLUMN + y) * RING + 2 * x_at + cs
            pl.when(comes[cs][k] & (low | to_self))(functools.partial(signal, source, k))
    each(RING, r, lambda i: signal(group * RING + i, q))
    each(KINDS, q, lambda i: signal(m, i))

    @pl.when(group < GROUPS - 1)
    def _():
        signal(jnp.where(group == COLUMN - 1, COLUMN * RING, m + RING), q)

    for copy in local[:3]:
        copy.wait()

    waves = tbuf[0].astype(f32)
    eye = lax.broadcasted_iota(jnp.int32, (OCT, OCT), 0) == lax.broadcasted_iota(jnp.int32, (OCT, OCT), 1)
    moves = jnp.sum(jnp.where(eye, ibuf[0].astype(f32), 0.0), axis=1, keepdims=True)
    masks = jnp.sum(jnp.where(eye, ibuf[1].astype(f32), 0.0), axis=1, keepdims=True)
    lane = lax.broadcasted_iota(jnp.int32, (OCT, 128), 1)
    tail = jnp.concatenate([waves[:, 256:], jnp.zeros((OCT, 128 - (L - 256)), f32)], axis=1)
    tail = jnp.where(lane == L - 256, moves, jnp.where(lane == L - 255, masks, tail))
    tail = jnp.concatenate([tail, jnp.zeros((OCT, 128), f32)], axis=1)
    msg[...] = jnp.concatenate([waves[:, :256], tail], axis=0).astype(bf16)

    @pl.when(group == GROUPS - 1)
    def _():
        xbuf[RING] = jnp.zeros((2, ROWS // 2, PIECE), bf16)

    count = (
        (COLUMN - 1) + 4 - to_self.astype(jnp.int32)
        + (RING - 1) + (KINDS - 1) + passes.astype(jnp.int32) + RING * head.astype(jnp.int32)
        + high * (5 + 8 * (1 - to_self.astype(jnp.int32)))
    )

    @pl.when(low)
    def _():
        all_ref[COLUMN:] = jnp.zeros((COLUMN, 8, 128), f32)

    pl.semaphore_wait(barrier, count)

    def answer(tm, tmpl):
        pl.semaphore_signal(ready, inc=1, device_id=(tm, tmpl), device_id_type=pl.DeviceIdType.MESH)

    @pl.when(high == 1)
    def _():
        answer(other, q)

    @pl.when((high == 1) & jnp.logical_not(to_self))
    def _():
        for cs in range(2):
            for k in range(KINDS):
                answer(y * RING + 2 * x_at + cs, k)

    def record(i):
        return rec_ref.at[pl.ds(2 * (2 * q + i % 2), 2), i // 2]

    def template_copy(i):
        return remote(msg, ybuf.at[y], w_send.at[i], w_recv.at[y], at_y(i), q)

    def pair_copy(i, z):
        return remote(
            pair.at[i], wbuf.at[KINDS * core + q], f_send.at[2 * i + z], f_recv.at[KINDS * core + q],
            *pair_target(i, z),
        )

    def record_copy(i):
        return remote(record(i), xbuf.at[r], x_send.at[i], x_recv.at[r], group * RING + i, q)

    def halo_copy():
        return remote(xbuf.at[0], xbuf.at[RING], h_send, x_recv.at[RING], m - RING, q)

    def edge_copy(i):
        return remote(record(i), xbuf.at[RING], e_send.at[i], x_recv.at[RING], (COLUMN - 1) * RING + i, q)

    def near_copy(i):
        return remote(all_ref.at[group], all_ref.at[group], s_send.at[i], s_recv.at[y], at_y(i), q)

    def far_copy():
        block = all_ref.at[pl.ds(COLUMN * high, COLUMN)]
        return remote(block, block, g_send, g_recv, other, q)

    def part_copy(i):
        me = KINDS * r + q
        return remote(
            part.at[i, pl.ds(0, 3)], land.at[me, pl.ds(0, 3)], p_send.at[i], p_recv.at[me], group * RING + i // KINDS, i % KINDS
        )

    goes = [[jnp.logical_not(to_self & (p % 4 == i) & (high == z)) for z in range(2)] for i in range(4)]

    each(COLUMN, y, lambda i: template_copy(i).start())

    @pl.when(head)
    def _():
        for i in range(RING):
            edge_copy(i).start()

    each(RING, r, lambda i: record_copy(i).start())
    ybuf[y] = msg[...]
    local[3].wait()
    each(RING, r, lambda i: remote(xbuf.at[i], xbuf.at[i], x_send.at[i], x_recv.at[i], m, q).wait_recv())

    @pl.when(passes)
    def _():
        halo_copy().start()

    main = jnp.concatenate([xbuf[i].astype(f32).reshape(ROWS, PIECE) for i in range(RING)], axis=1)
    all_ref[group] = block_sums(main, run_ref, sum_ref)
    each(COLUMN, y, lambda i: near_copy(i).start())

    each(COLUMN, y, lambda i: remote(msg, ybuf.at[i], w_send.at[i], w_recv.at[i], m, q).wait_recv())
    for i in range(4):
        both = [ybuf[2 * i + e].astype(f32) for e in range(2)]
        both = [jnp.concatenate([one[:OCT], one[OCT:, :128]], axis=1) for one in both]
        pair[i] = jnp.concatenate(both, axis=0).astype(bf16)
    for z in range(2):
        for i in range(4):
            pl.when(goes[i][z] & (high >= z))(lambda i=i, z=z: pair_copy(i, z).start())

    @pl.when(to_self)
    def _():
        wbuf[KINDS * core + q] = pair[p % 4]

    for j in range(SETS):
        shifted(j, main, h_ref, 0, EARLY)

    def near(i):
        block = all_ref.at[high * COLUMN + i]
        remote(block, block, s_send.at[i], s_recv.at[i], m, q).wait_recv()

    @pl.when(low)
    def _():
        each(COLUMN, y, near)
        pl.semaphore_wait(ready, 5)
        for i in range(4):
            pair_copy(i, 1).start()
        far_copy().start()

    @pl.when(group < GROUPS - 1)
    def _():
        remote(xbuf.at[0], xbuf.at[RING], h_send, x_recv.at[RING], m, q).wait_recv()

    halo = xbuf[RING].astype(f32).reshape(ROWS, PIECE)
    after = halo_sums(halo, run_ref, tail_ref)

    @pl.when(group == COLUMN - 1)
    def _():
        all_ref[COLUMN] = jnp.concatenate([after, jnp.zeros((7, 128), f32)], axis=0)

    ending = jnp.concatenate([main[:, EARLY:], halo, jnp.zeros((ROWS, NH - WIDE), f32)], axis=1)
    for j in range(SETS):
        shifted(j, ending, h_ref, EARLY, NH - EARLY)

    @pl.when(high == 1)
    def _():
        each(COLUMN, y, near)

    @pl.when(high == 1)
    def _():
        block = all_ref.at[pl.ds(0, COLUMN)]
        remote(block, block, g_send, g_recv, m, q).wait_recv()

    energy = window_energy(group, all_ref, run_ref, sum_ref, tail_ref, chain_ref, outer_ref, edge_ref, part_ref)
    root_ref[...] = 1.0 / jnp.sqrt(energy + EPS)

    for cs in range(2):
        for k in range(KINDS):
            slot = KINDS * cs + k
            pl.when(comes[cs][k])(
                lambda slot=slot: remote(
                    wbuf.at[slot], wbuf.at[slot], f_send.at[0], f_recv.at[slot], m, q
                ).wait_recv()
            )
    shards = wbuf[...].astype(f32)
    shards = [
        shards[KINDS * cs + k, OCT * e : OCT * e + OCT] for e in range(2) for cs in range(2) for k in range(KINDS)
    ]
    sel, weight = prepare(jnp.concatenate(shards, axis=0), a_ref)
    for j in range(SETS):
        correlate(j, h_ref, a_ref, z_ref, corr_ref)

    total = stacked(root_ref[...], weight, sel, corr_ref, n_ref, z_ref)
    for i in range(RING):
        for k in range(KINDS):
            for c in range(PIECE // 128):
                at = PIECE * i + 128 * c
                part[KINDS * i + k, c : c + 1, :] = total[k : k + 1, at : at + 128]

    me = KINDS * r + q
    each(RING * KINDS, me, lambda i: part_copy(i).start())
    land[me, :3] = part[me, :3]
    each(RING * KINDS, me, lambda i: remote(part.at[0, pl.ds(0, 3)], land.at[i, pl.ds(0, 3)], p_send.at[i], p_recv.at[i], m, q).wait_recv())
    whole = jnp.sum(land[:, :3], axis=0)
    for c in range(PIECE // 128):
        out_ref[:, 128 * c : 128 * c + 128] = whole[c : c + 1]

    each(COLUMN, y, lambda i: template_copy(i).wait_send())
    each(RING, r, lambda i: record_copy(i).wait_send())

    @pl.when(passes)
    def _():
        halo_copy().wait_send()

    @pl.when(head)
    def _():
        for i in range(RING):
            edge_copy(i).wait_send()

    for i in range(4):
        for z in range(2):
            pl.when(goes[i][z])(lambda i=i, z=z: pair_copy(i, z).wait_send())
    each(COLUMN, y, lambda i: near_copy(i).wait_send())

    @pl.when(low)
    def _():
        far_copy().wait_send()

    each(RING * KINDS, KINDS * r + q, lambda i: part_copy(i).wait_send())


def local(records, templates, shifts, valid):
    hbm = pl.BlockSpec(memory_space=pltpu.HBM)
    dma = pltpu.SemaphoreType.DMA
    return pl.pallas_call(
        kernel,
        out_shape=jax.ShapeDtypeStruct((1, PIECE), f32),
        in_specs=[hbm] * 4,
        out_specs=pl.BlockSpec(memory_space=pltpu.VMEM),
        scratch_shapes=[
            pltpu.VMEM((RING + 1, 2, ROWS // 2, PIECE), bf16),
            pltpu.VMEM((2 * KINDS, 16, 384), bf16),
            pltpu.VMEM((COLUMN, 16, 256), bf16),
            pltpu.VMEM((4, 16, 384), bf16),
            pltpu.VMEM((16, 256), bf16),
            pltpu.VMEM((GROUPS, 8, 128), f32),
            pltpu.VMEM((RING * KINDS, 8, 128), f32),
            pltpu.VMEM((RING * KINDS, 8, 128), f32),
            pltpu.VMEM((1, OCT, L), bf16),
            pltpu.VMEM((2, 1, OCT), jnp.int32),
            pltpu.VMEM((SETS, 256, NH), bf16),
            pltpu.VMEM((SETS, 128, BIG), bf16),
            pltpu.VMEM((2, 128, NZ), f32),
            pltpu.VMEM((256, NZ), bf16),
            pltpu.VMEM((128, NZ), f32),
            pltpu.VMEM((1280, 128), f32),
            pltpu.VMEM((128, 128), f32),
            pltpu.VMEM((128, 128), f32),
            pltpu.VMEM((256, 128), f32),
            pltpu.VMEM((256, 128), f32),
            pltpu.VMEM((256, 128), f32),
            pltpu.VMEM((128, 128), f32),
            pltpu.VMEM((ROWS, NZ), f32),
            dma((COLUMN,)), dma((COLUMN,)),
            dma((8,)), dma((2 * KINDS,)),
            dma((RING,)), dma((RING + 1,)), dma, dma((RING,)),
            dma((COLUMN,)), dma((COLUMN,)),
            dma, dma,
            dma((RING * KINDS,)), dma((RING * KINDS,)),
            dma((4,)),
            pltpu.SemaphoreType.REGULAR,
        ],
        compiler_params=pltpu.CompilerParams(
            collective_id=0, has_side_effects=True, vmem_limit_bytes=63 * 1024 * 1024
        ),
    )(records.reshape(GROUPS, 4, 16, PIECE), templates, shifts, valid)


def solution(mesh):
    in_specs = (P(None, "tm"), P("tmpl", "tm", None), P("tmpl", "tm"), P("tmpl", "tm"))
    return jax.shard_map(local, mesh=mesh, in_specs=in_specs, out_specs=P("tmpl", "tm"), check_vma=False)
```

```python
import functools

import jax
import jax.numpy as jnp
from jax import lax
from jax.experimental import pallas as pl
from jax.experimental.pallas import tpu as pltpu
from jax.sharding import PartitionSpec as P

L = 300
MAXS = 20
EPS = 1e-05
KINDS = 4
RING = 8
GROUPS = 16
COLUMN = 8
PIECE = 384
ROWS = 32
OCT = 8
SETS = ROWS // OCT
STEP = 32
SPAN = RING * PIECE
WIDE = SPAN + PIECE
NH = 3584
NZ = 3328
BIG = 3 * 256
QUARTER = SPAN // 4
EARLY = SPAN - 128
LEVELS = 22
BLOCKS = (WIDE // 16)
CHAIN = 208

f32 = jnp.float32
bf16 = jnp.bfloat16


def prepare(taps, a_ref):
    pairs = SETS * KINDS * OCT
    third = jnp.where(lax.broadcasted_iota(jnp.int32, (pairs, 128), 1) < L - 256, taps[:, 256:], 0.0)
    thirds = [taps[:, :128], taps[:, 128:256], third]

    parts = [part.astype(bf16) for part in thirds]
    lane = lax.broadcasted_iota(jnp.int32, (128, 256), 1)
    line = lax.broadcasted_iota(jnp.int32, (128, 256), 0)
    same = (lane % OCT) == (line % OCT)
    for u_lo in range(4):
        spread = jnp.where(line == STEP * u_lo + lane // OCT, 1.0, 0.0).astype(bf16)
        for u_hi in range(3):
            wide = jnp.dot(parts[u_hi], spread, preferred_element_type=f32)
            block = jnp.where(same, wide, 0.0).astype(bf16)
            for j in range(SETS):
                a_ref[j, 32 * u_lo : 32 * u_lo + 32, 256 * u_hi : 256 * u_hi + 256] = block[32 * j : 32 * j + 32]

    shift = taps[:, L : L + 1]
    valid = taps[:, L + 1 : L + 2]
    column = lax.broadcasted_iota(jnp.int32, (pairs, 128), 1)
    squares = thirds[0] ** 2 + thirds[1] ** 2 + thirds[2] ** 2
    power = jnp.sum(squares, axis=1, keepdims=True) / L
    weight = valid / (L * jnp.sqrt(power + EPS))

    kind = (lax.broadcasted_iota(jnp.int32, (pairs, 128), 0) // OCT) % KINDS
    picked = (shift == (column // KINDS).astype(f32)) & (kind == column % KINDS)
    sel = jnp.transpose(jnp.where(picked, 1.0, 0.0)).astype(bf16)
    return jnp.concatenate([sel, sel], axis=1)[: 4 * LEVELS], weight


def shifted(j, x, h_ref, start, keep):
    x8 = x[OCT * j : OCT * j + OCT]
    wide = x8.shape[1]
    for i in range(STEP // 2):
        first = x8 if i == 0 else pltpu.roll(x8, wide - 2 * i, 1)
        second = pltpu.roll(x8, wide - 2 * i - 1, 1)
        both = jnp.concatenate([first[:, :keep], second[:, :keep]], axis=0)
        h_ref[j, 16 * i : 16 * i + 16, start : start + keep] = both.astype(bf16)


def correlate(j, h_ref, a_ref, z_ref, corr_ref):
    slot = j % 2
    for n in range(NZ // 256):
        acc = None
        for u_hi in range(3):
            part = jnp.dot(
                a_ref[j, :, 256 * u_hi : 256 * u_hi + 256],
                h_ref[j, :, 256 * n + 128 * u_hi : 256 * n + 128 * u_hi + 256],
                preferred_element_type=f32,
            )
            acc = part if acc is None else acc + part
        z_ref[slot, :, 256 * n : 256 * n + 256] = acc
    for k in range(KINDS):
        corr = z_ref[slot, 8 * k : 8 * k + 8, :]
        for u_lo in range(1, 4):
            corr = corr + pltpu.roll(z_ref[slot, 32 * u_lo + 8 * k : 32 * u_lo + 8 * k + 8, :], NZ - STEP * u_lo, 1)
        corr_ref[32 * j + 8 * k : 32 * j + 8 * k + 8, :] = corr


def running16(run_ref, start, rows, sum_ref):
    acc = run_ref[pl.ds(start, rows, stride=16), :]
    for d in range(1, 16):
        acc = acc + run_ref[pl.ds(start + d, rows, stride=16), :]
        run_ref[pl.ds(start + d, rows, stride=16), :] = acc
    sum_ref[:rows, :] = acc
    sum_ref[rows:, :] = jnp.zeros((128 - rows, 128), f32)
    outer = sum_ref[pl.ds(0, 8, stride=16), :]
    for c in range(1, 16):
        outer = outer + sum_ref[pl.ds(c, 8, stride=16), :]
        sum_ref[pl.ds(c, 8, stride=16), :] = outer
    return acc, outer


def block_sums(x, run_ref, sum_ref):
    squares = x * x
    stacked = jnp.concatenate([squares[:, QUARTER * s : QUARTER * s + QUARTER] for s in range(4)], axis=0)
    for i in range(QUARTER // 128):
        run_ref[128 * i : 128 * i + 128, :] = jnp.transpose(stacked[:, 128 * i : 128 * i + 128])
    acc, outer = running16(run_ref, 0, QUARTER // 16, sum_ref)
    final = acc[QUARTER // 16 - 1 : QUARTER // 16]
    before = sum_ref[QUARTER // 16 - 2 : QUARTER // 16 - 1, :]
    return jnp.concatenate([outer[:3], final, before, jnp.zeros((3, 128), f32)], axis=0)


def halo_sums(x, run_ref, tail_ref):
    halo = jnp.concatenate([x * x, jnp.zeros((128 - ROWS, PIECE), f32)], axis=0)
    for i in range(PIECE // 128):
        run_ref[QUARTER + 128 * i : QUARTER + 128 * i + 128, :] = jnp.transpose(halo[:, 128 * i : 128 * i + 128])
    _, outer = running16(run_ref, QUARTER, PIECE // 16, tail_ref)
    return outer[:1]


def window_energy(group, all_ref, run_ref, sum_ref, tail_ref, chain_ref, outer_ref, edge_ref, part_ref):
    for g in range(GROUPS):
        totals = all_ref[g]
        for s in range(4):
            moved = totals if s == 0 else pltpu.roll(totals, 128 - ROWS * s, 1)
            chain_ref[12 * g + 3 * s : 12 * g + 3 * s + 3, :] = moved[:3]
    chain_ref[12 * GROUPS :, :] = jnp.zeros((256 - 12 * GROUPS, 128), f32)
    plain = chain_ref[:CHAIN, :]
    acc = chain_ref[pl.ds(0, 16, stride=16), :]
    for b in range(1, 16):
        acc = acc + chain_ref[pl.ds(b, 16, stride=16), :]
        chain_ref[pl.ds(b, 16, stride=16), :] = acc
    outer_ref[:8, :] = jnp.zeros((8, 128), f32)
    top = jnp.zeros((1, 128), f32)
    for a in range(CHAIN // 16):
        outer_ref[16 * a + 9 : 16 * a + 25, :] = chain_ref[16 * a : 16 * a + 16, :] + top
        top = top + acc[a : a + 1]
    outer_ref[8:9, :] = jnp.zeros((1, 128), f32)
    edge_ref[:8, :] = jnp.zeros((8, 128), f32)
    edge_ref[9 : 9 + CHAIN, :] = plain + outer_ref[8 : 8 + CHAIN, :]
    edge_ref[8:9, :] = jnp.zeros((1, 128), f32)
    mine = outer_ref[7:23, :]
    edge = edge_ref[7:23, :]
    for g in range(1, GROUPS):
        here = group == g
        mine = jnp.where(here, outer_ref[12 * g + 7 : 12 * g + 23, :], mine)
        edge = jnp.where(here, edge_ref[12 * g + 7 : 12 * g + 23, :], edge)
    lane = lax.broadcasted_iota(jnp.int32, (1, 128), 1) // ROWS

    def spread(rows, b):
        out = rows[1 + b : 2 + b]
        for s in range(1, 4):
            out = jnp.where(lane == s, pltpu.roll(rows[1 + 3 * s + b : 2 + 3 * s + b], ROWS * s, 1), out)
        return out

    befores = [spread(mine, b) for b in range(3)] + [mine[13:14], mine[14:15]]
    edges = [spread(edge, b) for b in range(3)] + [edge[13:14], edge[14:15]]
    for b in range(5):
        sums = sum_ref[16 * b : 16 * b + 16, :] if b < 3 else tail_ref[16 * b - 48 : 16 * b - 32, :]
        part_ref[16 * b + 1 : 16 * b + 17, :] = sums + befores[b]
        part_ref[16 * b : 16 * b + 1, :] = edges[b]
    quarter = QUARTER
    rows = (quarter + PIECE) // 16
    base = part_ref[:rows, :]
    for d in range(16):
        run_ref[pl.ds(d, rows, stride=16), :] = run_ref[pl.ds(d, rows, stride=16), :] + base
    ahead = pltpu.roll(all_ref[jnp.maximum(group - 1, 0)], ROWS, 1)
    last = jnp.where(group > 0, ahead[3:4] + (ahead[4:5] + mine[0:1]), 0.0)
    stretch = quarter + PIECE
    run_ref[stretch : stretch + 128, :] = jnp.concatenate([jnp.zeros((127, 128), f32), last], axis=0)
    main = jnp.concatenate(
        [jnp.transpose(run_ref[128 * i : 128 * i + 128, :]) for i in range(quarter // 128)], axis=1
    )
    tail = [jnp.transpose(run_ref[quarter + 128 * i : quarter + 128 * i + 128, :])[:ROWS] for i in range(4)]
    running = jnp.concatenate([main[ROWS * s : ROWS * s + ROWS] for s in range(4)] + tail, axis=1)
    energy = pltpu.roll(running, NH - (L - 1), 1) - pltpu.roll(running, 1, 1)
    return jnp.maximum(energy, 0.0)[:, :NZ] / L


def stacked(inverse, weight, sel, corr_ref, n_ref, z_ref):
    pairs = SETS * KINDS * OCT
    for j in range(SETS):
        for k in range(KINDS):
            row = 32 * j + 8 * k
            corr_ref[row : row + 8, :] = corr_ref[row : row + 8, :] * inverse[OCT * j : OCT * j + OCT] * weight[row : row + 8]
        normed = corr_ref[32 * j : 32 * j + 32, :]
        head = normed.astype(bf16)
        n_ref[32 * j : 32 * j + 32, :] = head
        n_ref[pairs + 32 * j : pairs + 32 * j + 32, :] = (normed - head.astype(f32)).astype(bf16)
    for n in range(NZ // 256):
        z_ref[0, : 4 * LEVELS, 256 * n : 256 * n + 256] = jnp.dot(
            sel, n_ref[:, 256 * n : 256 * n + 256], preferred_element_type=f32
        )
    total = z_ref[0, :8, :]
    for i in range(1, LEVELS // 2):
        total = total + pltpu.roll(z_ref[0, 8 * i : 8 * i + 8, :], NZ - 2 * i, 1)
    return total + pltpu.roll(pltpu.roll(total, NZ - 1, 1), 4, 0)


def kernel(
    rec_ref, tmpl_ref, shift_ref, valid_ref, out_ref,
    xbuf, wbuf, ybuf, pair, msg, all_ref, part, land, tbuf, ibuf,
    h_ref, a_ref, z_ref, n_ref, corr_ref, run_ref, sum_ref, tail_ref, chain_ref, outer_ref, edge_ref, part_ref, root_ref,
    w_send, w_recv, f_send, f_recv, x_send, x_recv, h_send, e_send, s_send, s_recv, g_send, g_recv,
    p_send, p_recv, own, ready,
):
    m, q = lax.axis_index("tm"), lax.axis_index("tmpl")
    group, r = m // RING, m % RING
    high, y = group // COLUMN, group % COLUMN
    x_at, core = r // 2, r % 2
    p = 2 * q + core
    to_self = p // 4 == high
    barrier = pltpu.get_barrier_semaphore()

    def signal(tm, tmpl):
        pl.semaphore_signal(barrier, inc=1, device_id=(tm, tmpl), device_id_type=pl.DeviceIdType.MESH)

    def remote(src, dst, send, recv, tm, tmpl):
        return pltpu.make_async_remote_copy(
            src_ref=src, dst_ref=dst, send_sem=send, recv_sem=recv,
            device_id=(tm, tmpl), device_id_type=pl.DeviceIdType.MESH,
        )

    def each(count, skip, step):
        for i in range(count):
            pl.when(i != skip)(functools.partial(step, i))

    def at_y(i):
        return (high * COLUMN + i) * RING + r

    local = [
        pltpu.make_async_copy(tmpl_ref, tbuf, own.at[0]),
        pltpu.make_async_copy(shift_ref, ibuf.at[0], own.at[1]),
        pltpu.make_async_copy(valid_ref, ibuf.at[1], own.at[2]),
        pltpu.make_async_copy(rec_ref.at[pl.ds(2 * p, 2), x_at], xbuf.at[r], own.at[3]),
    ]
    for copy in local:
        copy.start()

    low = high == 0
    passes = (group > 0) & (group != COLUMN)
    head = m == COLUMN * RING
    other = (1 - high) * COLUMN * RING + y * RING + r

    def pair_target(i, z):
        return (z * COLUMN + y) * RING + 2 * x_at + i % 2, 2 * high + i // 2

    @pl.when(low)
    def _():
        signal(other, q)
        for i in range(4):
            signal(*pair_target(i, 1))

    each(COLUMN, y, lambda i: signal(at_y(i), q))
    comes = [
        [jnp.logical_not(to_self & (core == cs) & (q == k)) for k in range(KINDS)] for cs in range(2)
    ]
    for cs in range(2):
        for k in range(KINDS):
            source = ((p // 4) * COLUMN + y) * RING + 2 * x_at + cs
            pl.when(comes[cs][k] & (low | to_self))(functools.partial(signal, source, k))
    each(RING, r, lambda i: signal(group * RING + i, q))
    each(KINDS, q, lambda i: signal(m, i))

    @pl.when(group < GROUPS - 1)
    def _():
        signal(jnp.where(group == COLUMN - 1, COLUMN * RING, m + RING), q)

    for copy in local[:3]:
        copy.wait()

    waves = tbuf[0].astype(f32)
    eye = lax.broadcasted_iota(jnp.int32, (OCT, OCT), 0) == lax.broadcasted_iota(jnp.int32, (OCT, OCT), 1)
    moves = jnp.sum(jnp.where(eye, ibuf[0].astype(f32), 0.0), axis=1, keepdims=True)
    masks = jnp.sum(jnp.where(eye, ibuf[1].astype(f32), 0.0), axis=1, keepdims=True)
    lane = lax.broadcasted_iota(jnp.int32, (OCT, 128), 1)
    tail = jnp.concatenate([waves[:, 256:], jnp.zeros((OCT, 128 - (L - 256)), f32)], axis=1)
    tail = jnp.where(lane == L - 256, moves, jnp.where(lane == L - 255, masks, tail))
    tail = jnp.concatenate([tail, jnp.zeros((OCT, 128), f32)], axis=1)
    msg[...] = jnp.concatenate([waves[:, :256], tail], axis=0).astype(bf16)

    @pl.when(group == GROUPS - 1)
    def _():
        xbuf[RING] = jnp.zeros((2, ROWS // 2, PIECE), bf16)

    count = (
        (COLUMN - 1) + 4 - to_self.astype(jnp.int32)
        + (RING - 1) + (KINDS - 1) + passes.astype(jnp.int32) + RING * head.astype(jnp.int32)
        + high * (5 + 8 * (1 - to_self.astype(jnp.int32)))
    )

    @pl.when(low)
    def _():
        all_ref[COLUMN:] = jnp.zeros((COLUMN, 8, 128), f32)

    pl.semaphore_wait(barrier, count)

    def answer(tm, tmpl):
        pl.semaphore_signal(ready, inc=1, device_id=(tm, tmpl), device_id_type=pl.DeviceIdType.MESH)

    @pl.when(high == 1)
    def _():
        answer(other, q)

    @pl.when((high == 1) & jnp.logical_not(to_self))
    def _():
        for cs in range(2):
            for k in range(KINDS):
                answer(y * RING + 2 * x_at + cs, k)

    def record(i):
        return rec_ref.at[pl.ds(2 * (2 * q + i % 2), 2), i // 2]

    def template_copy(i):
        return remote(msg, ybuf.at[y], w_send.at[i], w_recv.at[y], at_y(i), q)

    def pair_copy(i, z):
        return remote(
            pair.at[i], wbuf.at[KINDS * core + q], f_send.at[2 * i + z], f_recv.at[KINDS * core + q],
            *pair_target(i, z),
        )

    def record_copy(i):
        return remote(record(i), xbuf.at[r], x_send.at[i], x_recv.at[r], group * RING + i, q)

    def halo_copy():
        return remote(xbuf.at[0], xbuf.at[RING], h_send, x_recv.at[RING], m - RING, q)

    def edge_copy(i):
        return remote(record(i), xbuf.at[RING], e_send.at[i], x_recv.at[RING], (COLUMN - 1) * RING + i, q)

    def near_copy(i):
        return remote(all_ref.at[group], all_ref.at[group], s_send.at[i], s_recv.at[y], at_y(i), q)

    def far_copy():
        block = all_ref.at[pl.ds(COLUMN * high, COLUMN)]
        return remote(block, block, g_send, g_recv, other, q)

    def part_copy(i):
        me = KINDS * r + q
        return remote(
            part.at[i, pl.ds(0, 3)], land.at[me, pl.ds(0, 3)], p_send.at[i], p_recv.at[me], group * RING + i // KINDS, i % KINDS
        )

    goes = [[jnp.logical_not(to_self & (p % 4 == i) & (high == z)) for z in range(2)] for i in range(4)]

    each(COLUMN, y, lambda i: template_copy(i).start())

    @pl.when(head)
    def _():
        for i in range(RING):
            edge_copy(i).start()

    each(RING, r, lambda i: record_copy(i).start())
    ybuf[y] = msg[...]
    local[3].wait()

    each(COLUMN, y, lambda i: remote(msg, ybuf.at[i], w_send.at[i], w_recv.at[i], m, q).wait_recv())
    for i in range(4):
        both = [ybuf[2 * i + e].astype(f32) for e in range(2)]
        both = [jnp.concatenate([one[:OCT], one[OCT:, :128]], axis=1) for one in both]
        pair[i] = jnp.concatenate(both, axis=0).astype(bf16)
    for z in range(2):
        for i in range(4):
            pl.when(goes[i][z] & (high >= z))(lambda i=i, z=z: pair_copy(i, z).start())

    @pl.when(to_self)
    def _():
        wbuf[KINDS * core + q] = pair[p % 4]

    each(RING, r, lambda i: remote(xbuf.at[i], xbuf.at[i], x_send.at[i], x_recv.at[i], m, q).wait_recv())

    @pl.when(passes)
    def _():
        halo_copy().start()

    main = jnp.concatenate([xbuf[i].astype(f32).reshape(ROWS, PIECE) for i in range(RING)], axis=1)
    all_ref[group] = block_sums(main, run_ref, sum_ref)
    each(COLUMN, y, lambda i: near_copy(i).start())

    for j in range(SETS):
        shifted(j, main, h_ref, 0, EARLY)

    def near(i):
        block = all_ref.at[high * COLUMN + i]
        remote(block, block, s_send.at[i], s_recv.at[i], m, q).wait_recv()

    @pl.when(low)
    def _():
        each(COLUMN, y, near)
        pl.semaphore_wait(ready, 5)
        for i in range(4):
            pair_copy(i, 1).start()
        far_copy().start()

    @pl.when(group < GROUPS - 1)
    def _():
        remote(xbuf.at[0], xbuf.at[RING], h_send, x_recv.at[RING], m, q).wait_recv()

    halo = xbuf[RING].astype(f32).reshape(ROWS, PIECE)
    after = halo_sums(halo, run_ref, tail_ref)

    @pl.when(group == COLUMN - 1)
    def _():
        all_ref[COLUMN] = jnp.concatenate([after, jnp.zeros((7, 128), f32)], axis=0)

    ending = jnp.concatenate([main[:, EARLY:], halo, jnp.zeros((ROWS, NH - WIDE), f32)], axis=1)
    for j in range(SETS):
        shifted(j, ending, h_ref, EARLY, NH - EARLY)

    @pl.when(high == 1)
    def _():
        each(COLUMN, y, near)

    @pl.when(high == 1)
    def _():
        block = all_ref.at[pl.ds(0, COLUMN)]
        remote(block, block, g_send, g_recv, m, q).wait_recv()

    energy = window_energy(group, all_ref, run_ref, sum_ref, tail_ref, chain_ref, outer_ref, edge_ref, part_ref)
    root_ref[...] = 1.0 / jnp.sqrt(energy + EPS)

    for cs in range(2):
        for k in range(KINDS):
            slot = KINDS * cs + k
            pl.when(comes[cs][k])(
                lambda slot=slot: remote(
                    wbuf.at[slot], wbuf.at[slot], f_send.at[0], f_recv.at[slot], m, q
                ).wait_recv()
            )
    shards = wbuf[...].astype(f32)
    shards = [
        shards[KINDS * cs + k, OCT * e : OCT * e + OCT] for e in range(2) for cs in range(2) for k in range(KINDS)
    ]
    sel, weight = prepare(jnp.concatenate(shards, axis=0), a_ref)
    for j in range(SETS):
        correlate(j, h_ref, a_ref, z_ref, corr_ref)

    total = stacked(root_ref[...], weight, sel, corr_ref, n_ref, z_ref)
    for i in range(RING):
        for k in range(KINDS):
            for c in range(PIECE // 128):
                at = PIECE * i + 128 * c
                part[KINDS * i + k, c : c + 1, :] = total[k : k + 1, at : at + 128]

    me = KINDS * r + q
    each(RING * KINDS, me, lambda i: part_copy(i).start())
    land[me, :3] = part[me, :3]
    each(RING * KINDS, me, lambda i: remote(part.at[0, pl.ds(0, 3)], land.at[i, pl.ds(0, 3)], p_send.at[i], p_recv.at[i], m, q).wait_recv())
    whole = jnp.sum(land[:, :3], axis=0)
    for c in range(PIECE // 128):
        out_ref[:, 128 * c : 128 * c + 128] = whole[c : c + 1]

    each(COLUMN, y, lambda i: template_copy(i).wait_send())
    each(RING, r, lambda i: record_copy(i).wait_send())

    @pl.when(passes)
    def _():
        halo_copy().wait_send()

    @pl.when(head)
    def _():
        for i in range(RING):
            edge_copy(i).wait_send()

    for i in range(4):
        for z in range(2):
            pl.when(goes[i][z])(lambda i=i, z=z: pair_copy(i, z).wait_send())
    each(COLUMN, y, lambda i: near_copy(i).wait_send())

    @pl.when(low)
    def _():
        far_copy().wait_send()

    each(RING * KINDS, KINDS * r + q, lambda i: part_copy(i).wait_send())


def local(records, templates, shifts, valid):
    hbm = pl.BlockSpec(memory_space=pltpu.HBM)
    dma = pltpu.SemaphoreType.DMA
    return pl.pallas_call(
        kernel,
        out_shape=jax.ShapeDtypeStruct((1, PIECE), f32),
        in_specs=[hbm] * 4,
        out_specs=pl.BlockSpec(memory_space=pltpu.VMEM),
        scratch_shapes=[
            pltpu.VMEM((RING + 1, 2, ROWS // 2, PIECE), bf16),
            pltpu.VMEM((2 * KINDS, 16, 384), bf16),
            pltpu.VMEM((COLUMN, 16, 256), bf16),
            pltpu.VMEM((4, 16, 384), bf16),
            pltpu.VMEM((16, 256), bf16),
            pltpu.VMEM((GROUPS, 8, 128), f32),
            pltpu.VMEM((RING * KINDS, 8, 128), f32),
            pltpu.VMEM((RING * KINDS, 8, 128), f32),
            pltpu.VMEM((1, OCT, L), bf16),
            pltpu.VMEM((2, 1, OCT), jnp.int32),
            pltpu.VMEM((SETS, 256, NH), bf16),
            pltpu.VMEM((SETS, 128, BIG), bf16),
            pltpu.VMEM((2, 128, NZ), f32),
            pltpu.VMEM((256, NZ), bf16),
            pltpu.VMEM((128, NZ), f32),
            pltpu.VMEM((1280, 128), f32),
            pltpu.VMEM((128, 128), f32),
            pltpu.VMEM((128, 128), f32),
            pltpu.VMEM((256, 128), f32),
            pltpu.VMEM((256, 128), f32),
            pltpu.VMEM((256, 128), f32),
            pltpu.VMEM((128, 128), f32),
            pltpu.VMEM((ROWS, NZ), f32),
            dma((COLUMN,)), dma((COLUMN,)),
            dma((8,)), dma((2 * KINDS,)),
            dma((RING,)), dma((RING + 1,)), dma, dma((RING,)),
            dma((COLUMN,)), dma((COLUMN,)),
            dma, dma,
            dma((RING * KINDS,)), dma((RING * KINDS,)),
            dma((4,)),
            pltpu.SemaphoreType.REGULAR,
        ],
        compiler_params=pltpu.CompilerParams(
            collective_id=0, has_side_effects=True, vmem_limit_bytes=63 * 1024 * 1024
        ),
    )(records.reshape(GROUPS, 4, 16, PIECE), templates, shifts, valid)


def solution(mesh):
    in_specs = (P(None, "tm"), P("tmpl", "tm", None), P("tmpl", "tm"), P("tmpl", "tm"))
    return jax.shard_map(local, mesh=mesh, in_specs=in_specs, out_specs=P("tmpl", "tm"), check_vma=False)
```
